128 devices in a mesh: dp: 64 (over y, x, z), feat: 2 (over core).
Axes of the slice: x: 4, y: 4, z: 4, core: 2. Of those that a mesh axis runs over, the one named last changes fastest.
Arguments:
- view_one: float32 [1024, 8192], P('dp', 'feat'), may hold values from -30 to 30, as said below
- view_two: float32 [1024, 8192], P('dp', 'feat'), may hold values from -30 to 30, as said below
- loss_scale: float32 [1], replicated, may hold values from 512 to 4096
Outputs:
- grad_one: float32 [1024, 8192], P('dp', 'feat')
- grad_two: float32 [1024, 8192], P('dp', 'feat')
The draws below stay inside these ranges and needn't reach their ends.
Inputs may be any that keep to these rules, and one draw needn't show every extreme that they name: `view_one`: float embeddings. `view_two`: float embeddings.
All inputs are finite; a program needn't handle non-finite values.
Results may differ from the reference program's by a relative error of at most 0.008.
Values may be sent and summed in bfloat16 or wider, within the bound.
A program may use at most 128 MiB of HBM per device.

```python
import math
import jax
import jax.numpy as jnp
from jax import lax

F = 8192
SAMPLES = 1024


def common_parts(key):
    key_a, key_b, key_c, key_d = jax.random.split(key, 4)
    shared = jax.random.normal(key_a, (SAMPLES, F), jnp.float32)
    factors = jax.random.normal(key_b, (SAMPLES, 4), jnp.float32)
    loads = 0.2 * jax.random.normal(key_c, (4, F), jnp.float32)
    scales = jnp.exp(jax.random.uniform(key_d, (F,), jnp.float32, math.log(0.3), math.log(3.0)))
    mixed = factors[:, 0:1] * loads[0] + factors[:, 1:2] * loads[1]
    mixed = mixed + factors[:, 2:3] * loads[2] + factors[:, 3:4] * loads[3]
    return (shared + mixed, scales)


def draw_view_one(key, part):
    base, scales = common_parts(key)
    key = jax.random.fold_in(key, 11)
    noise = 0.7 * jax.random.normal(key, (SAMPLES, F), jnp.float32)
    return jnp.clip(scales * (base + noise), -30.0, 30.0)


def draw_view_two(key, part):
    base, scales = common_parts(key)
    key = jax.random.fold_in(key, 23)
    noise = 0.7 * jax.random.normal(key, (SAMPLES, F), jnp.float32)
    return jnp.clip(scales * (base + noise), -30.0, 30.0)


def setup_inputs(seed: int = 0) -> dict:
    seeds = jax.random.split(jax.random.key(seed), 4)
    return {
        "view_one": draw_view_one(jax.random.fold_in(seeds[3], 71), 0),
        "view_two": draw_view_two(jax.random.fold_in(seeds[3], 71), 0),
        "loss_scale": jnp.clip(jnp.exp(jax.random.uniform(seeds[2], (1,), jnp.float32, math.log(512.0), math.log(4096.0))), 512.0, 4096.0),
    }


eps_value = 1e-05
offdiag_weight = 0.0051

def normalize(view):
    centre = view - lax.optimization_barrier(jnp.mean(view, axis=0))
    variance = lax.optimization_barrier(jnp.mean(centre * centre, axis=0))
    inverse = lax.rsqrt(variance + eps_value)
    return ((centre * inverse).astype(jnp.bfloat16), inverse)

def finish(back, normal, inverse):
    normal_f = normal.astype(jnp.float32)
    weight = lax.optimization_barrier(jnp.mean(back * normal_f, axis=0))
    return inverse * (back - normal_f * weight)

def reference(view_one, view_two, loss_scale):
    samples = view_one.shape[0]
    normal_one, inverse_one = normalize(view_one)
    normal_two, inverse_two = normalize(view_two)
    corr = lax.dot_general(normal_one, normal_two, (((0,), (0,)), ((), ())), preferred_element_type=jnp.float32) / samples
    on_diag = jnp.eye(corr.shape[0], dtype=bool)
    grad_corr = (loss_scale[0] * jnp.where(on_diag, 2.0 * (corr - 1.0), 2.0 * offdiag_weight * corr)).astype(jnp.bfloat16)
    back_one = lax.dot_general(normal_two, grad_corr, (((1,), (1,)), ((), ())), preferred_element_type=jnp.float32) / samples
    back_two = jnp.dot(normal_one, grad_corr, preferred_element_type=jnp.float32) / samples
    return (finish(back_one, normal_one, inverse_one), finish(back_two, normal_two, inverse_two))
```

```python
import jax
import jax.numpy as jnp
from jax import lax
from jax.experimental import pallas as pl
from jax.experimental.pallas import tpu as pltpu
from jax.sharding import PartitionSpec as P

MESH = pl.DeviceIdType.MESH
F32, BF16 = jnp.float32, jnp.bfloat16

eps_value = 1e-05
offdiag_weight = 0.0051

CHIPS, CORES = 64, 2
SAMPLES, ROWS, WIDE, TILE = 1024, 16, 4096, 128
BLOCKS = [(r, c) for r in range(8) for c in range(r, 8)]
PART = len(BLOCKS) * TILE // 3
THIRD, FINE = PART // 4, PART // 16
ORDERS = ((4, 16, 1), (16, 1, 4), (1, 4, 16))


def remote(src, dst, send_sem, recv_sem, chip, core):
    return pltpu.make_async_remote_copy(
        src_ref=src, dst_ref=dst, send_sem=send_sem, recv_sem=recv_sem, device_id=(chip, core), device_id_type=MESH
    )


def rows_at(start, size):
    return pl.ds(pl.multiple_of(start, 16), size)


def lanes_at(tile):
    return pl.ds(pl.multiple_of(tile * TILE, TILE), TILE)


def coordinate(chip, stride):
    return (chip // stride) % 4


def partner(chip, stride, hop):
    here = coordinate(chip, stride)
    return chip + ((here + hop) % 4 - here) * stride


def kernel(
    one, two, scale_ref, out, held, own, other, inv_own, inv_other, part, got_a, sum_a, got_b, sum_b, got_c, full, gram, grads,
    in_send, in_recv, out_send, out_recv, pair_send, pair_recv, ring_send, ring_recv, local_sem,
):
    chip, core = lax.axis_index("dp"), lax.axis_index("feat")
    half, tile = chip // 32, chip % 32
    mine = half == core

    barrier = pltpu.get_barrier_semaphore()

    @pl.loop(1, CHIPS * CORES)
    def _(k):
        flat = (chip * CORES + core + k) % (CHIPS * CORES)
        pl.semaphore_signal(barrier, inc=1, device_id=(flat // CORES, flat % CORES), device_id_type=MESH)

    pl.semaphore_wait(barrier, CHIPS * CORES - 1)

    def to_owner(t, view, target_core):
        chip_to = 32 * core + t
        return remote(
            view.at[:, lanes_at(t)], held.at[rows_at(chip * ROWS, ROWS), :],
            in_send.at[2 * t + target_core], in_recv.at[chip], chip_to, target_core,
        )

    def stays(t, target_core):
        return jnp.logical_and(32 * core + t == chip, core == target_core)

    @pl.loop(0, 32)
    def _(k):
        t = (k + chip) % 32
        for target_core, view in enumerate((one, two)):
            @pl.when(jnp.logical_not(stays(t, target_core)))
            def _():
                to_owner(t, view, target_core).start()

            @pl.when(stays(t, target_core))
            def _():
                pltpu.make_async_copy(view.at[:, lanes_at(t)], held.at[rows_at(chip * ROWS, ROWS), :], local_sem).start()

    @pl.when(mine)
    def _():
        pltpu.make_async_copy(one.at[:, lanes_at(tile)], held.at[rows_at(chip * ROWS, ROWS), :], local_sem).wait()

    @pl.loop(0, CHIPS)
    def _(i):
        @pl.when(jnp.logical_not(jnp.logical_and(i == chip, mine)))
        def _():
            rows = held.at[rows_at(i * ROWS, ROWS), :]
            remote(rows, rows, in_send.at[0], in_recv.at[i], chip, core).wait_recv()

    values = held[...]
    centre = values - jnp.sum(values, axis=0, keepdims=True) / SAMPLES
    variance = jnp.sum(centre * centre, axis=0, keepdims=True) / SAMPLES
    inverse = lax.rsqrt(variance + eps_value)
    own[...] = (centre * inverse).astype(BF16)
    inv_own[...] = jnp.broadcast_to(inverse, inv_own.shape)
    swap = remote(own, other, pair_send.at[0], pair_recv.at[0], chip, 1 - core)
    swap_inv = remote(inv_own, inv_other, pair_send.at[1], pair_recv.at[1], chip, 1 - core)
    swap.start()
    swap_inv.start()

    for r in range(8):
        panel = lax.dot_general(
            own[r * TILE:(r + 1) * TILE, :], own[r * TILE:, :], (((1,), (1,)), ((), ())), preferred_element_type=F32
        )
        for c in range(r, 8):
            at = BLOCKS.index((r, c)) * TILE
            part[at:at + TILE, :] = panel[:, (c - r) * TILE:(c - r + 1) * TILE].astype(BF16)

    def step(phase, p, hop, src, dst):
        stride = ORDERS[p][(0, 1, 2, 1, 0)[phase]]
        at = (phase * 3 + p) * 3 + hop - 1
        return remote(src, dst, ring_send.at[at], ring_recv.at[at], partner(chip, stride, hop), core)

    def first(p, hop):
        to = (coordinate(chip, ORDERS[p][0]) + hop) % 4
        return step(0, p, hop, part.at[rows_at(p * PART + to * THIRD, THIRD), :], got_a.at[p, hop - 1])

    def second(p, hop):
        to = (coordinate(chip, ORDERS[p][1]) + hop) % 4
        return step(1, p, hop, sum_a.at[p, rows_at(to * FINE, FINE), :], got_b.at[p, hop - 1])

    def third(p, hop):
        return step(2, p, hop, sum_b.at[p], got_c.at[p, hop - 1])

    def fine_rows(p):
        start = p * PART + coordinate(chip, ORDERS[p][0]) * THIRD + coordinate(chip, ORDERS[p][1]) * FINE
        return rows_at(start, FINE)

    def third_rows(p):
        return rows_at(p * PART + coordinate(chip, ORDERS[p][0]) * THIRD, THIRD)

    def fourth(p, hop):
        return step(3, p, hop, full.at[fine_rows(p), :], full.at[fine_rows(p), :])

    def fifth(p, hop):
        return step(4, p, hop, full.at[third_rows(p), :], full.at[third_rows(p), :])

    HOPS = (2, 1, 3)
    for p in range(3):
        for hop in HOPS:
            first(p, hop).start()
    for p in range(3):
        for hop in HOPS:
            first(p, hop).wait_recv()
        total = part[third_rows(p), :].astype(F32)
        for hop in HOPS:
            total = total + got_a[p, hop - 1].astype(F32)
        sum_a[p] = total.astype(BF16)
        for hop in HOPS:
            second(p, hop).start()
    for p in range(3):
        for hop in HOPS:
            second(p, hop).wait_recv()
        total = sum_a[p, rows_at(coordinate(chip, ORDERS[p][1]) * FINE, FINE), :].astype(F32)
        for hop in HOPS:
            total = total + got_b[p, hop - 1].astype(F32)
        sum_b[p] = total.astype(BF16)
        for hop in HOPS:
            third(p, hop).start()
    for p in range(3):
        for hop in HOPS:
            third(p, hop).wait_recv()
        total = sum_b[p].astype(F32)
        for hop in HOPS:
            total = total + got_c[p, hop - 1].astype(F32)
        full[fine_rows(p), :] = total.astype(BF16)
        for hop in HOPS:
            fourth(p, hop).start()
    for p in range(3):
        for hop in HOPS:
            fourth(p, hop).wait_recv()
        for hop in HOPS:
            fifth(p, hop).start()

    swap.wait_recv()
    swap_inv.wait_recv()
    theirs = other[...].astype(F32)
    ours = own[...].astype(F32)
    scale = scale_ref[0]
    corr = jnp.sum(ours * theirs, axis=0, keepdims=True) / SAMPLES
    diagonal = scale * (2.0 * (corr - 1.0) - 2.0 * offdiag_weight * corr)

    for p in range(3):
        for hop in HOPS:
            fifth(p, hop).wait_recv()
    for at, (r, c) in enumerate(BLOCKS):
        block = full[at * TILE:(at + 1) * TILE, :]
        gram[r * TILE:(r + 1) * TILE, c * TILE:(c + 1) * TILE] = block
        if r != c:
            gram[c * TILE:(c + 1) * TILE, r * TILE:(r + 1) * TILE] = block.T
    back = jnp.dot(gram[...], other[...], preferred_element_type=F32) * (scale * (2.0 * offdiag_weight / (SAMPLES * SAMPLES)))
    back = back + ours * (diagonal / SAMPLES)
    weight = jnp.sum(back * theirs, axis=0, keepdims=True) / SAMPLES
    grads[...] = (inv_other[0:1, :] * (back - theirs * weight)).astype(BF16)

    def to_samples(i):
        return remote(
            grads.at[rows_at(i * ROWS, ROWS), :], out.at[1 - core, :, lanes_at(tile)],
            out_send.at[i], out_recv.at[2 * tile + core], i, half,
        )

    @pl.loop(0, CHIPS)
    def _(k):
        i = (k + chip) % CHIPS
        stay = jnp.logical_and(i == chip, mine)

        @pl.when(jnp.logical_not(stay))
        def _():
            to_samples(i).start()

        @pl.when(stay)
        def _():
            pltpu.make_async_copy(grads.at[rows_at(i * ROWS, ROWS), :], out.at[1 - core, :, lanes_at(tile)], local_sem).start()

    @pl.when(mine)
    def _():
        pltpu.make_async_copy(
            grads.at[rows_at(chip * ROWS, ROWS), :], out.at[1 - core, :, lanes_at(tile)], local_sem
        ).wait()

    @pl.loop(0, 32)
    def _(t):
        for from_core in range(2):
            @pl.when(jnp.logical_not(stays(t, from_core)))
            def _():
                remote(
                    grads.at[rows_at(0, ROWS), :], out.at[1 - from_core, :, lanes_at(t)],
                    out_send.at[0], out_recv.at[2 * t + from_core], chip, core,
                ).wait_recv()

    swap.wait_send()
    swap_inv.wait_send()
    for p in range(3):
        for hop in HOPS:
            for send in (first, second, third, fourth, fifth):
                send(p, hop).wait_send()

    @pl.loop(0, 32)
    def _(t):
        for target_core, view in enumerate((one, two)):
            @pl.when(jnp.logical_not(stays(t, target_core)))
            def _():
                to_owner(t, view, target_core).wait_send()

    @pl.loop(0, CHIPS)
    def _(i):
        @pl.when(jnp.logical_not(jnp.logical_and(i == chip, mine)))
        def _():
            to_samples(i).wait_send()


def shards(view_one, view_two, loss_scale):
    out = pl.pallas_call(
        kernel,
        out_shape=jax.ShapeDtypeStruct((2, ROWS, WIDE), BF16),
        in_specs=[
            pl.BlockSpec(memory_space=pl.ANY),
            pl.BlockSpec(memory_space=pl.ANY),
            pl.BlockSpec(memory_space=pltpu.SMEM),
        ],
        out_specs=pl.BlockSpec(memory_space=pltpu.VMEM),
        scratch_shapes=[
            pltpu.VMEM((SAMPLES, TILE), F32),
            pltpu.VMEM((SAMPLES, TILE), BF16),
            pltpu.VMEM((SAMPLES, TILE), BF16),
            pltpu.VMEM((8, TILE), F32),
            pltpu.VMEM((8, TILE), F32),
            pltpu.VMEM((3 * PART, TILE), BF16),
            pltpu.VMEM((3, 3, THIRD, TILE), BF16),
            pltpu.VMEM((3, THIRD, TILE), BF16),
            pltpu.VMEM((3, 3, FINE, TILE), BF16),
            pltpu.VMEM((3, FINE, TILE), BF16),
            pltpu.VMEM((3, 3, FINE, TILE), BF16),
            pltpu.VMEM((3 * PART, TILE), BF16),
            pltpu.VMEM((SAMPLES, SAMPLES), BF16),
            pltpu.VMEM((SAMPLES, TILE), BF16),
            pltpu.SemaphoreType.DMA((CHIPS,)),
            pltpu.SemaphoreType.DMA((CHIPS,)),
            pltpu.SemaphoreType.DMA((CHIPS,)),
            pltpu.SemaphoreType.DMA((CHIPS,)),
            pltpu.SemaphoreType.DMA((2,)),
            pltpu.SemaphoreType.DMA((2,)),
            pltpu.SemaphoreType.DMA((45,)),
            pltpu.SemaphoreType.DMA((45,)),
            pltpu.SemaphoreType.DMA,
        ],
        compiler_params=pltpu.CompilerParams(
            collective_id=0, has_side_effects=True, vmem_limit_bytes=40 * 1024 * 1024
        ),
    )(view_one, view_two, loss_scale)
    return out[0].astype(F32), out[1].astype(F32)


def solution(mesh):
    placed = (P("dp", "feat"), P("dp", "feat"), P())
    return jax.shard_map(
        shards,
        mesh=mesh,
        in_specs=placed,
        out_specs=(P("dp", "feat"), P("dp", "feat")),
        check_vma=False,
    )
```

```python
import jax
import jax.numpy as jnp
from jax import lax
from jax.experimental import pallas as pl
from jax.experimental.pallas import tpu as pltpu
from jax.sharding import PartitionSpec as P

MESH = pl.DeviceIdType.MESH
F32, BF16 = jnp.float32, jnp.bfloat16

eps_value = 1e-05
offdiag_weight = 0.0051

CHIPS = 64
SAMPLES, ROWS, WIDE, TILE = 1024, 16, 4096, 128
BLOCKS = [(r, c) for r in range(8) for c in range(r, 8)]
WAVES = 2
CHAINS = 3 * WAVES
PART = len(BLOCKS) * TILE // CHAINS
CHUNK, FINE = PART // 4, PART // 16
ORDERS = ((4, 16, 1), (16, 1, 4), (1, 4, 16))
HOPS = (2, 1, 3)
PHASES = 5


def apart(shift):
    return min(shift, 4 - shift)


SHIFTS = sorted(
    ((y, x, z) for y in range(4) for x in range(4) for z in range(4)), key=lambda s: -(apart(s[0]) + apart(s[1]) + apart(s[2]))
)
PLANE = [(x, z) for y, x, z in SHIFTS if y == 0]


def remote(src, dst, send_sem, recv_sem, chip, core):
    return pltpu.make_async_remote_copy(
        src_ref=src, dst_ref=dst, send_sem=send_sem, recv_sem=recv_sem, device_id=(chip, core), device_id_type=MESH
    )


def rows_at(start, size):
    return pl.ds(pl.multiple_of(start, 16), size)


def lanes_at(tile):
    return pl.ds(pl.multiple_of(tile * TILE, TILE), TILE)


def coordinate(chip, stride):
    return (chip // stride) % 4


def partner(chip, stride, hop):
    here = coordinate(chip, stride)
    return chip + ((here + hop) % 4 - here) * stride


def kernel(
    one, two, scale_hbm, out, held, own, other, inv_own, inv_other, part, got_a, sum_a, got_b, sum_b, got_c, full, gram, grads,
    scale_ref, in_send, in_recv, out_send, out_recv, pair_send, pair_recv, ring_send, ring_recv, local_sem, scale_sem,
):
    chip, core = lax.axis_index("dp"), lax.axis_index("feat")
    half, tile = chip // 32, chip % 32
    mine = half == core
    not_mine = jnp.logical_not(mine)
    at_y, at_x, at_z = coordinate(chip, 16), coordinate(chip, 4), coordinate(chip, 1)

    def shifted(shift):
        y, x, z = shift
        return (at_y + y) % 4 * 16 + (at_x + x) % 4 * 4 + (at_z + z) % 4

    barrier = pltpu.get_barrier_semaphore()
    for shift in SHIFTS[:-1]:
        pl.semaphore_signal(barrier, inc=1, device_id=(shifted(shift), half), device_id_type=MESH)

    @pl.when(not_mine)
    def _():
        pl.semaphore_signal(barrier, inc=1, device_id=(chip, half), device_id_type=MESH)

    scale_copy = pltpu.make_async_copy(scale_hbm, scale_ref, scale_sem)
    scale_copy.start()

    @pl.when(mine)
    def _():
        pl.semaphore_wait(barrier, CHIPS - 1)

    @pl.when(not_mine)
    def _():
        pl.semaphore_wait(barrier, CHIPS)

    my_rows = held.at[rows_at(chip * ROWS, ROWS), :]

    def to_owner(view, chip_to, core_to):
        return remote(view.at[:, lanes_at(chip_to % 32)], my_rows, in_send, in_recv, chip_to, core_to)

    for x, z in PLANE[:-1]:
        for y in range(2):
            chip_to = (2 * core + y) * 16 + (at_x + x) % 4 * 4 + (at_z + z) % 4
            to_owner(one, chip_to, 0).start()
            to_owner(two, chip_to, 1).start()
    for y in range(2):
        chip_to = (2 * core + y) * 16 + at_x * 4 + at_z
        for core_to, view in enumerate((one, two)):
            stays = jnp.logical_and(chip_to == chip, core == core_to)

            @pl.when(jnp.logical_not(stays))
            def _():
                to_owner(view, chip_to, core_to).start()

            @pl.when(stays)
            def _():
                pltpu.make_async_copy(view.at[:, lanes_at(tile)], my_rows, local_sem).start()

    def all_of(ref, count, send_sem, recv_sem):
        rows = ref.at[0:count * ROWS, :]
        return remote(rows, rows, send_sem, recv_sem, chip, core)

    def local_in():
        return pltpu.make_async_copy(one.at[:, lanes_at(tile)], my_rows, local_sem)

    @pl.when(mine)
    def _():
        all_of(held, CHIPS - 1, in_send, in_recv).wait_recv()
        local_in().wait()

    @pl.when(not_mine)
    def _():
        all_of(held, CHIPS, in_send, in_recv).wait_recv()

    values = held[...]
    centre = values - jnp.sum(values, axis=0, keepdims=True) / SAMPLES
    variance = jnp.sum(centre * centre, axis=0, keepdims=True) / SAMPLES
    inverse = lax.rsqrt(variance + eps_value)
    own[...] = (centre * inverse).astype(BF16)
    inv_own[...] = jnp.broadcast_to(inverse, inv_own.shape)
    swap = remote(own, other, pair_send.at[0], pair_recv.at[0], chip, 1 - core)
    swap_inv = remote(inv_own, inv_other, pair_send.at[1], pair_recv.at[1], chip, 1 - core)

    def step(phase, q, hop, src, dst):
        stride = ORDERS[q % 3][(0, 1, 2, 1, 0)[phase]]
        at = (phase * CHAINS + q) * 3 + hop - 1
        return remote(src, dst, ring_send.at[at], ring_recv.at[at], partner(chip, stride, hop), core)

    def first(q, hop):
        to = (coordinate(chip, ORDERS[q % 3][0]) + hop) % 4
        return step(0, q, hop, part.at[rows_at(q * PART + to * CHUNK, CHUNK), :], got_a.at[q, hop - 1])

    def second(q, hop):
        to = (coordinate(chip, ORDERS[q % 3][1]) + hop) % 4
        return step(1, q, hop, sum_a.at[q, rows_at(to * FINE, FINE), :], got_b.at[q, hop - 1])

    def third(q, hop):
        return step(2, q, hop, sum_b.at[q], got_c.at[q, hop - 1])

    def chunk_rows(q):
        return rows_at(q * PART + coordinate(chip, ORDERS[q % 3][0]) * CHUNK, CHUNK)

    def fine_rows(q):
        start = q * PART + coordinate(chip, ORDERS[q % 3][0]) * CHUNK + coordinate(chip, ORDERS[q % 3][1]) * FINE
        return rows_at(start, FINE)

    def fourth(q, hop):
        return step(3, q, hop, full.at[fine_rows(q), :], full.at[fine_rows(q), :])

    def fifth(q, hop):
        return step(4, q, hop, full.at[chunk_rows(q), :], full.at[chunk_rows(q), :])

    def chains(wave):
        return range(3 * wave, 3 * wave + 3)

    def start(phase, q):
        for hop in HOPS:
            phase(q, hop).start()

    def arrived(phase, q):
        for hop in HOPS:
            phase(q, hop).wait_recv()

    def summed(mine_ref, got, q):
        total = mine_ref.astype(F32)
        for hop in HOPS:
            total = total + got[q, hop - 1].astype(F32)
        return total.astype(BF16)


    def sent_in():
        @pl.when(mine)
        def _():
            all_of(held, CHIPS - 1, in_send, in_recv).wait_send()

        @pl.when(not_mine)
        def _():
            all_of(held, CHIPS, in_send, in_recv).wait_send()

    swap.start()
    swap_inv.start()

    for wave in range(WAVES):
        blocks = list(enumerate(BLOCKS))[wave * 36 // WAVES:(wave + 1) * 36 // WAVES]
        for r in range(8):
            columns = [c for _, (row, c) in blocks if row == r]
            if columns:
                panel = lax.dot_general(
                    own[r * TILE:(r + 1) * TILE, :], own[columns[0] * TILE:(columns[-1] + 1) * TILE, :],
                    (((1,), (1,)), ((), ())), preferred_element_type=F32,
                )
                for at, (row, c) in blocks:
                    if row == r:
                        lanes = slice((c - columns[0]) * TILE, (c - columns[0] + 1) * TILE)
                        part[at * TILE:(at + 1) * TILE, :] = panel[:, lanes].astype(BF16)
        for q in chains(wave):
            start(first, q)

    sent_in()
    swap.wait()
    swap_inv.wait()
    scale_copy.wait()
    scale = scale_ref[0]
    corr = jnp.sum(own[...].astype(F32) * other[...].astype(F32), axis=0, keepdims=True) / SAMPLES
    diagonal = scale * (2.0 * (corr - 1.0) - 2.0 * offdiag_weight * corr)

    for wave in range(WAVES):
        for q in chains(wave):
            arrived(first, q)
            sum_a[q] = summed(part[chunk_rows(q), :], got_a, q)
            start(second, q)
    for wave in range(WAVES):
        for q in chains(wave):
            arrived(second, q)
            sum_b[q] = summed(sum_a[q, rows_at(coordinate(chip, ORDERS[q % 3][1]) * FINE, FINE), :], got_b, q)
            start(third, q)
    for wave in range(WAVES):
        for q in chains(wave):
            arrived(third, q)
            full[fine_rows(q), :] = summed(sum_b[q], got_c, q)
            start(fourth, q)
    for wave in range(WAVES):
        for q in chains(wave):
            arrived(fourth, q)
            start(fifth, q)

    for wave in range(WAVES):
        for q in chains(wave):
            arrived(fifth, q)
        for at, (r, c) in list(enumerate(BLOCKS))[wave * 36 // WAVES:(wave + 1) * 36 // WAVES]:
            block = full[at * TILE:(at + 1) * TILE, :]
            gram[r * TILE:(r + 1) * TILE, c * TILE:(c + 1) * TILE] = block
            if r != c:
                gram[c * TILE:(c + 1) * TILE, r * TILE:(r + 1) * TILE] = block.T
    theirs = other[...].astype(F32)
    back = jnp.dot(gram[...], other[...], preferred_element_type=F32) * (scale * (2.0 * offdiag_weight / (SAMPLES * SAMPLES)))
    back = back + own[...].astype(F32) * (diagonal / SAMPLES)
    weight = jnp.sum(back * theirs, axis=0, keepdims=True) / SAMPLES
    grads[...] = (inv_other[0:1, :] * (back - theirs * weight)).astype(BF16)

    place = out.at[1 - core, :, lanes_at(tile)]

    def to_samples(chip_to):
        return remote(grads.at[rows_at(chip_to * ROWS, ROWS), :], place, out_send, out_recv, chip_to, half)

    for shift in SHIFTS[:-1]:
        to_samples(shifted(shift)).start()

    @pl.when(not_mine)
    def _():
        to_samples(chip).start()

    @pl.when(mine)
    def _():
        pltpu.make_async_copy(grads.at[rows_at(chip * ROWS, ROWS), :], place, local_sem).start()

    for phase in (first, second, third, fourth, fifth):
        for q in range(CHAINS):
            for hop in HOPS:
                phase(q, hop).wait_send()

    @pl.when(mine)
    def _():
        all_of(grads, CHIPS - 1, out_send, out_recv).wait()
        pltpu.make_async_copy(grads.at[rows_at(chip * ROWS, ROWS), :], place, local_sem).wait()

    @pl.when(not_mine)
    def _():
        all_of(grads, CHIPS, out_send, out_recv).wait()


def shards(view_one, view_two, loss_scale):
    hbm = pl.BlockSpec(memory_space=pltpu.HBM)
    out = pl.pallas_call(
        kernel,
        out_shape=jax.ShapeDtypeStruct((2, ROWS, WIDE), BF16),
        in_specs=[hbm, hbm, hbm],
        out_specs=pl.BlockSpec(memory_space=pltpu.VMEM),
        scratch_shapes=[
            pltpu.VMEM((SAMPLES, TILE), F32),
            pltpu.VMEM((SAMPLES, TILE), BF16),
            pltpu.VMEM((SAMPLES, TILE), BF16),
            pltpu.VMEM((8, TILE), F32),
            pltpu.VMEM((8, TILE), F32),
            pltpu.VMEM((CHAINS * PART, TILE), BF16),
            pltpu.VMEM((CHAINS, 3, CHUNK, TILE), BF16),
            pltpu.VMEM((CHAINS, CHUNK, TILE), BF16),
            pltpu.VMEM((CHAINS, 3, FINE, TILE), BF16),
            pltpu.VMEM((CHAINS, FINE, TILE), BF16),
            pltpu.VMEM((CHAINS, 3, FINE, TILE), BF16),
            pltpu.VMEM((CHAINS * PART, TILE), BF16),
            pltpu.VMEM((SAMPLES, SAMPLES), BF16),
            pltpu.VMEM((SAMPLES, TILE), BF16),
            pltpu.SMEM((1,), F32),
            pltpu.SemaphoreType.DMA,
            pltpu.SemaphoreType.DMA,
            pltpu.SemaphoreType.DMA,
            pltpu.SemaphoreType.DMA,
            pltpu.SemaphoreType.DMA((2,)),
            pltpu.SemaphoreType.DMA((2,)),
            pltpu.SemaphoreType.DMA((PHASES * CHAINS * 3,)),
            pltpu.SemaphoreType.DMA((PHASES * CHAINS * 3,)),
            pltpu.SemaphoreType.DMA,
            pltpu.SemaphoreType.DMA,
        ],
        compiler_params=pltpu.CompilerParams(
            collective_id=0, has_side_effects=True, vmem_limit_bytes=60 * 1024 * 1024
        ),
    )(view_one, view_two, loss_scale)
    return out[0].astype(F32), out[1].astype(F32)


def solution(mesh):
    placed = (P("dp", "feat"), P("dp", "feat"), P())
    return jax.shard_map(
        shards,
        mesh=mesh,
        in_specs=placed,
        out_specs=(P("dp", "feat"), P("dp", "feat")),
        check_vma=False,
    )
```

```python
import jax
import jax.numpy as jnp
from jax import lax
from jax.experimental import pallas as pl
from jax.experimental.pallas import tpu as pltpu
from jax.sharding import PartitionSpec as P

MESH = pl.DeviceIdType.MESH
F32, BF16 = jnp.float32, jnp.bfloat16

eps_value = 1e-05
offdiag_weight = 0.0051

CHIPS = 64
SAMPLES, ROWS, WIDE, TILE = 1024, 16, 4096, 128
BLOCKS = [(r, c) for r in range(8) for c in range(r, 8)]
WAVES = 2
CHAINS = 3 * WAVES
PART = len(BLOCKS) * TILE // CHAINS
CHUNK, FINE = PART // 4, PART // 16
ORDERS = ((4, 16, 1), (16, 1, 4), (1, 4, 16))
HOPS = (2, 1, 3)
PHASES = 5


def apart(shift):
    return min(shift, 4 - shift)


SHIFTS = sorted(
    ((y, x, z) for y in range(4) for x in range(4) for z in range(4)), key=lambda s: -(apart(s[0]) + apart(s[1]) + apart(s[2]))
)
PLANE = [(x, z) for y, x, z in SHIFTS if y == 0]


def remote(src, dst, send_sem, recv_sem, chip, core):
    return pltpu.make_async_remote_copy(
        src_ref=src, dst_ref=dst, send_sem=send_sem, recv_sem=recv_sem, device_id=(chip, core), device_id_type=MESH
    )


def rows_at(start, size):
    return pl.ds(pl.multiple_of(start, 16), size)


def lanes_at(tile):
    return pl.ds(pl.multiple_of(tile * TILE, TILE), TILE)


def coordinate(chip, stride):
    return (chip // stride) % 4


def partner(chip, stride, hop):
    here = coordinate(chip, stride)
    return chip + ((here + hop) % 4 - here) * stride


def kernel(
    one, two, scale_hbm, out, views, means, rests, held, held_means, own, other, inv_own, inv_other, part, got_a, sum_a, got_b, sum_b, got_c, full, gram, grads,
    scale_ref, in_send, in_recv, mean_send, mean_recv, out_send, out_recv, pair_send, pair_recv, ring_send, ring_recv, local_sem, view_sem, scale_sem,
):
    chip, core = lax.axis_index("dp"), lax.axis_index("feat")
    half, tile = chip // 32, chip % 32
    mine = half == core
    not_mine = jnp.logical_not(mine)
    at_y, at_x, at_z = coordinate(chip, 16), coordinate(chip, 4), coordinate(chip, 1)

    def shifted(shift):
        y, x, z = shift
        return (at_y + y) % 4 * 16 + (at_x + x) % 4 * 4 + (at_z + z) % 4

    loads = [pltpu.make_async_copy(view, views.at[k], view_sem.at[k]) for k, view in enumerate((one, two))]
    for load in loads:
        load.start()

    barrier = pltpu.get_barrier_semaphore()
    for shift in SHIFTS[:-1]:
        pl.semaphore_signal(barrier, inc=1, device_id=(shifted(shift), half), device_id_type=MESH)

    @pl.when(not_mine)
    def _():
        pl.semaphore_signal(barrier, inc=1, device_id=(chip, half), device_id_type=MESH)

    scale_copy = pltpu.make_async_copy(scale_hbm, scale_ref, scale_sem)
    scale_copy.start()

    for k, load in enumerate(loads):
        load.wait()
        samples = views[k]
        block_mean = jnp.sum(samples, axis=0, keepdims=True) / ROWS
        rests[k] = (samples - block_mean).astype(BF16)
        for t in range(WIDE // TILE):
            means[k, t] = block_mean[:, t * TILE:(t + 1) * TILE]

    @pl.when(mine)
    def _():
        pl.semaphore_wait(barrier, CHIPS - 1)

    @pl.when(not_mine)
    def _():
        pl.semaphore_wait(barrier, CHIPS)

    my_rows = held.at[rows_at(chip * ROWS, ROWS), :]

    def to_owner(chip_to, core_to):
        t = chip_to % 32
        return (
            remote(means.at[core_to, t], held_means.at[chip], mean_send, mean_recv, chip_to, core_to),
            remote(rests.at[core_to, :, lanes_at(t)], my_rows, in_send, in_recv, chip_to, core_to),
        )

    def stay_here():
        return (
            pltpu.make_async_copy(means.at[core, tile], held_means.at[chip], local_sem.at[0]),
            pltpu.make_async_copy(rests.at[core, :, lanes_at(tile)], my_rows, local_sem.at[1]),
        )

    for x, z in PLANE[:-1]:
        for y in range(2):
            chip_to = (2 * core + y) * 16 + (at_x + x) % 4 * 4 + (at_z + z) % 4
            for core_to in range(2):
                for copy in to_owner(chip_to, core_to):
                    copy.start()
    for y in range(2):
        chip_to = (2 * core + y) * 16 + at_x * 4 + at_z
        for core_to in range(2):
            stays = jnp.logical_and(chip_to == chip, core == core_to)

            @pl.when(jnp.logical_not(stays))
            def _():
                for copy in to_owner(chip_to, core_to):
                    copy.start()

            @pl.when(stays)
            def _():
                for copy in stay_here():
                    copy.start()

    def all_of(ref, count, send_sem, recv_sem):
        rows = ref.at[0:count]
        return remote(rows, rows, send_sem, recv_sem, chip, core)

    def all_in(count):
        return all_of(held_means, count, mean_send, mean_recv), all_of(held, count * ROWS, in_send, in_recv)

    @pl.when(mine)
    def _():
        for copy in all_in(CHIPS - 1):
            copy.wait_recv()
        for copy in stay_here():
            copy.wait()

    @pl.when(not_mine)
    def _():
        for copy in all_in(CHIPS):
            copy.wait_recv()

    block_means = held_means[...]
    offsets = block_means - jnp.sum(block_means, axis=0, keepdims=True) / CHIPS
    centre = (held[...].astype(F32).reshape(CHIPS, ROWS, TILE) + offsets).reshape(SAMPLES, TILE)
    variance = jnp.sum(centre * centre, axis=0, keepdims=True) / SAMPLES
    inverse = lax.rsqrt(variance + eps_value)
    own[...] = (centre * inverse).astype(BF16)
    inv_own[...] = jnp.broadcast_to(inverse, inv_own.shape)
    swap = remote(own, other, pair_send.at[0], pair_recv.at[0], chip, 1 - core)
    swap_inv = remote(inv_own, inv_other, pair_send.at[1], pair_recv.at[1], chip, 1 - core)

    def step(phase, q, hop, src, dst):
        stride = ORDERS[q % 3][(0, 1, 2, 1, 0)[phase]]
        at = (phase * CHAINS + q) * 3 + hop - 1
        return remote(src, dst, ring_send.at[at], ring_recv.at[at], partner(chip, stride, hop), core)

    def first(q, hop):
        to = (coordinate(chip, ORDERS[q % 3][0]) + hop) % 4
        return step(0, q, hop, part.at[rows_at(q * PART + to * CHUNK, CHUNK), :], got_a.at[q, hop - 1])

    def second(q, hop):
        to = (coordinate(chip, ORDERS[q % 3][1]) + hop) % 4
        return step(1, q, hop, sum_a.at[q, rows_at(to * FINE, FINE), :], got_b.at[q, hop - 1])

    def third(q, hop):
        return step(2, q, hop, sum_b.at[q], got_c.at[q, hop - 1])

    def chunk_rows(q):
        return rows_at(q * PART + coordinate(chip, ORDERS[q % 3][0]) * CHUNK, CHUNK)

    def fine_rows(q):
        start = q * PART + coordinate(chip, ORDERS[q % 3][0]) * CHUNK + coordinate(chip, ORDERS[q % 3][1]) * FINE
        return rows_at(start, FINE)

    def fourth(q, hop):
        return step(3, q, hop, full.at[fine_rows(q), :], full.at[fine_rows(q), :])

    def fifth(q, hop):
        return step(4, q, hop, full.at[chunk_rows(q), :], full.at[chunk_rows(q), :])

    def chains(wave):
        return range(3 * wave, 3 * wave + 3)

    def start(phase, q):
        for hop in HOPS:
            phase(q, hop).start()

    def arrived(phase, q):
        for hop in HOPS:
            phase(q, hop).wait_recv()

    def summed(mine_ref, got, q):
        total = mine_ref.astype(F32)
        for hop in HOPS:
            total = total + got[q, hop - 1].astype(F32)
        return total.astype(BF16)


    def sent_in():
        @pl.when(mine)
        def _():
            for copy in all_in(CHIPS - 1):
                copy.wait_send()

        @pl.when(not_mine)
        def _():
            for copy in all_in(CHIPS):
                copy.wait_send()

    swap.start()
    swap_inv.start()

    for wave in range(WAVES):
        blocks = list(enumerate(BLOCKS))[wave * 36 // WAVES:(wave + 1) * 36 // WAVES]
        for r in range(8):
            columns = [c for _, (row, c) in blocks if row == r]
            if columns:
                panel = lax.dot_general(
                    own[r * TILE:(r + 1) * TILE, :], own[columns[0] * TILE:(columns[-1] + 1) * TILE, :],
                    (((1,), (1,)), ((), ())), preferred_element_type=F32,
                )
                for at, (row, c) in blocks:
                    if row == r:
                        lanes = slice((c - columns[0]) * TILE, (c - columns[0] + 1) * TILE)
                        part[at * TILE:(at + 1) * TILE, :] = panel[:, lanes].astype(BF16)
        for q in chains(wave):
            start(first, q)

    sent_in()
    swap.wait()
    swap_inv.wait()
    scale_copy.wait()
    scale = scale_ref[0]
    corr = jnp.sum(own[...].astype(F32) * other[...].astype(F32), axis=0, keepdims=True) / SAMPLES
    diagonal = scale * (2.0 * (corr - 1.0) - 2.0 * offdiag_weight * corr)

    for wave in range(WAVES):
        for q in chains(wave):
            arrived(first, q)
            sum_a[q] = summed(part[chunk_rows(q), :], got_a, q)
            start(second, q)
    for wave in range(WAVES):
        for q in chains(wave):
            arrived(second, q)
            sum_b[q] = summed(sum_a[q, rows_at(coordinate(chip, ORDERS[q % 3][1]) * FINE, FINE), :], got_b, q)
            start(third, q)
    for wave in range(WAVES):
        for q in chains(wave):
            arrived(third, q)
            full[fine_rows(q), :] = summed(sum_b[q], got_c, q)
            start(fourth, q)
    for wave in range(WAVES):
        for q in chains(wave):
            arrived(fourth, q)
            start(fifth, q)

    for wave in range(WAVES):
        for q in chains(wave):
            arrived(fifth, q)
        for at, (r, c) in list(enumerate(BLOCKS))[wave * 36 // WAVES:(wave + 1) * 36 // WAVES]:
            block = full[at * TILE:(at + 1) * TILE, :]
            gram[r * TILE:(r + 1) * TILE, c * TILE:(c + 1) * TILE] = block
            if r != c:
                gram[c * TILE:(c + 1) * TILE, r * TILE:(r + 1) * TILE] = block.T
    theirs = other[...].astype(F32)
    back = jnp.dot(gram[...], other[...], preferred_element_type=F32) * (scale * (2.0 * offdiag_weight / (SAMPLES * SAMPLES)))
    back = back + own[...].astype(F32) * (diagonal / SAMPLES)
    weight = jnp.sum(back * theirs, axis=0, keepdims=True) / SAMPLES
    grads[...] = (inv_other[0:1, :] * (back - theirs * weight)).astype(BF16)

    place = out.at[1 - core, :, lanes_at(tile)]

    def to_samples(chip_to):
        return remote(grads.at[rows_at(chip_to * ROWS, ROWS), :], place, out_send, out_recv, chip_to, half)

    for shift in SHIFTS[:-1]:
        to_samples(shifted(shift)).start()

    @pl.when(not_mine)
    def _():
        to_samples(chip).start()

    @pl.when(mine)
    def _():
        pltpu.make_async_copy(grads.at[rows_at(chip * ROWS, ROWS), :], place, local_sem.at[0]).start()

    for phase in (first, second, third, fourth, fifth):
        for q in range(CHAINS):
            for hop in HOPS:
                phase(q, hop).wait_send()

    @pl.when(mine)
    def _():
        all_of(grads, (CHIPS - 1) * ROWS, out_send, out_recv).wait()
        pltpu.make_async_copy(grads.at[rows_at(chip * ROWS, ROWS), :], place, local_sem.at[0]).wait()

    @pl.when(not_mine)
    def _():
        all_of(grads, CHIPS * ROWS, out_send, out_recv).wait()


def shards(view_one, view_two, loss_scale):
    hbm = pl.BlockSpec(memory_space=pltpu.HBM)
    out = pl.pallas_call(
        kernel,
        out_shape=jax.ShapeDtypeStruct((2, ROWS, WIDE), BF16),
        in_specs=[hbm, hbm, hbm],
        out_specs=pl.BlockSpec(memory_space=pltpu.VMEM),
        scratch_shapes=[
            pltpu.VMEM((2, ROWS, WIDE), F32),
            pltpu.VMEM((2, WIDE // TILE, 1, TILE), F32),
            pltpu.VMEM((2, ROWS, WIDE), BF16),
            pltpu.VMEM((SAMPLES, TILE), BF16),
            pltpu.VMEM((CHIPS, 1, TILE), F32),
            pltpu.VMEM((SAMPLES, TILE), BF16),
            pltpu.VMEM((SAMPLES, TILE), BF16),
            pltpu.VMEM((8, TILE), F32),
            pltpu.VMEM((8, TILE), F32),
            pltpu.VMEM((CHAINS * PART, TILE), BF16),
            pltpu.VMEM((CHAINS, 3, CHUNK, TILE), BF16),
            pltpu.VMEM((CHAINS, CHUNK, TILE), BF16),
            pltpu.VMEM((CHAINS, 3, FINE, TILE), BF16),
            pltpu.VMEM((CHAINS, FINE, TILE), BF16),
            pltpu.VMEM((CHAINS, 3, FINE, TILE), BF16),
            pltpu.VMEM((CHAINS * PART, TILE), BF16),
            pltpu.VMEM((SAMPLES, SAMPLES), BF16),
            pltpu.VMEM((SAMPLES, TILE), BF16),
            pltpu.SMEM((1,), F32),
            pltpu.SemaphoreType.DMA,
            pltpu.SemaphoreType.DMA,
            pltpu.SemaphoreType.DMA,
            pltpu.SemaphoreType.DMA,
            pltpu.SemaphoreType.DMA,
            pltpu.SemaphoreType.DMA,
            pltpu.SemaphoreType.DMA((2,)),
            pltpu.SemaphoreType.DMA((2,)),
            pltpu.SemaphoreType.DMA((PHASES * CHAINS * 3,)),
            pltpu.SemaphoreType.DMA((PHASES * CHAINS * 3,)),
            pltpu.SemaphoreType.DMA((2,)),
            pltpu.SemaphoreType.DMA((2,)),
            pltpu.SemaphoreType.DMA,
        ],
        compiler_params=pltpu.CompilerParams(
            collective_id=0, has_side_effects=True, vmem_limit_bytes=54848 * 1024
        ),
    )(view_one, view_two, loss_scale)
    return out[0].astype(F32), out[1].astype(F32)


def solution(mesh):
    placed = (P("dp", "feat"), P("dp", "feat"), P())
    return jax.shard_map(
        shards,
        mesh=mesh,
        in_specs=placed,
        out_specs=(P("dp", "feat"), P("dp", "feat")),
        check_vma=False,
    )
```

```python
import jax
import jax.numpy as jnp
from jax import lax
from jax.experimental import pallas as pl
from jax.experimental.pallas import tpu as pltpu
from jax.sharding import PartitionSpec as P

MESH = pl.DeviceIdType.MESH
F32, BF16 = jnp.float32, jnp.bfloat16

eps_value = 1e-05
offdiag_weight = 0.0051

CHIPS = 64
SAMPLES, ROWS, WIDE, TILE = 1024, 16, 4096, 128
BLOCKS = [(r, c) for r in range(8) for c in range(r, 8)]
WAVES = 3
CHAINS = 3 * WAVES
WHOLE = [0] + [min(r for r, c in BLOCKS[wave * 36 // WAVES:] + [(8, 8)]) * TILE for wave in range(1, WAVES + 1)]
PART = len(BLOCKS) * TILE // CHAINS
CHUNK, FINE = PART // 4, PART // 16
ORDERS = ((4, 16, 1), (16, 1, 4), (1, 4, 16))
HOPS = (2, 1, 3)
PHASES = 5


def apart(shift):
    return min(shift, 4 - shift)


SHIFTS = sorted(
    ((y, x, z) for y in range(4) for x in range(4) for z in range(4)), key=lambda s: -(apart(s[0]) + apart(s[1]) + apart(s[2]))
)
PLANE = [(x, z) for y, x, z in SHIFTS if y == 0]


def remote(src, dst, send_sem, recv_sem, chip, core):
    return pltpu.make_async_remote_copy(
        src_ref=src, dst_ref=dst, send_sem=send_sem, recv_sem=recv_sem, device_id=(chip, core), device_id_type=MESH
    )


def rows_at(start, size):
    return pl.ds(pl.multiple_of(start, 16), size)


def lanes_at(tile):
    return pl.ds(pl.multiple_of(tile * TILE, TILE), TILE)


def coordinate(chip, stride):
    return (chip // stride) % 4


def partner(chip, stride, hop):
    here = coordinate(chip, stride)
    return chip + ((here + hop) % 4 - here) * stride


def kernel(
    one, two, scale_hbm, out, views, means, rests, held, held_means, own, other, inv_own, inv_other, part, got_a, sum_a, got_b, sum_b, got_c, full, gram, products, grads,
    scale_ref, in_send, in_recv, mean_send, mean_recv, out_send, out_recv, pair_send, pair_recv, ring_send, ring_recv, local_sem, view_sem, scale_sem,
):
    chip, core = lax.axis_index("dp"), lax.axis_index("feat")
    half, tile = chip // 32, chip % 32
    mine = half == core
    not_mine = jnp.logical_not(mine)
    at_y, at_x, at_z = coordinate(chip, 16), coordinate(chip, 4), coordinate(chip, 1)

    def shifted(shift):
        y, x, z = shift
        return (at_y + y) % 4 * 16 + (at_x + x) % 4 * 4 + (at_z + z) % 4

    loads = [pltpu.make_async_copy(view, views.at[k], view_sem.at[k]) for k, view in enumerate((one, two))]
    for load in loads:
        load.start()

    barrier = pltpu.get_barrier_semaphore()
    for shift in SHIFTS[:-1]:
        pl.semaphore_signal(barrier, inc=1, device_id=(shifted(shift), half), device_id_type=MESH)

    @pl.when(not_mine)
    def _():
        pl.semaphore_signal(barrier, inc=1, device_id=(chip, half), device_id_type=MESH)

    scale_copy = pltpu.make_async_copy(scale_hbm, scale_ref, scale_sem)
    scale_copy.start()

    for k, load in enumerate(loads):
        load.wait()
        samples = views[k]
        block_mean = jnp.sum(samples, axis=0, keepdims=True) / ROWS
        rests[k] = (samples - block_mean).astype(BF16)
        for t in range(WIDE // TILE):
            means[k, t] = block_mean[:, t * TILE:(t + 1) * TILE]

    @pl.when(mine)
    def _():
        pl.semaphore_wait(barrier, CHIPS - 1)

    @pl.when(not_mine)
    def _():
        pl.semaphore_wait(barrier, CHIPS)

    my_rows = held.at[rows_at(chip * ROWS, ROWS), :]

    def to_owner(chip_to, core_to):
        t = chip_to % 32
        return (
            remote(means.at[core_to, t], held_means.at[chip], mean_send, mean_recv, chip_to, core_to),
            remote(rests.at[core_to, :, lanes_at(t)], my_rows, in_send, in_recv, chip_to, core_to),
        )

    def stay_here():
        return (
            pltpu.make_async_copy(means.at[core, tile], held_means.at[chip], local_sem.at[0]),
            pltpu.make_async_copy(rests.at[core, :, lanes_at(tile)], my_rows, local_sem.at[1]),
        )

    for x, z in PLANE[:-1]:
        for y in range(2):
            chip_to = (2 * core + y) * 16 + (at_x + x) % 4 * 4 + (at_z + z) % 4
            for core_to in range(2):
                for copy in to_owner(chip_to, core_to):
                    copy.start()
    for y in range(2):
        chip_to = (2 * core + y) * 16 + at_x * 4 + at_z
        for core_to in range(2):
            stays = jnp.logical_and(chip_to == chip, core == core_to)

            @pl.when(jnp.logical_not(stays))
            def _():
                for copy in to_owner(chip_to, core_to):
                    copy.start()

            @pl.when(stays)
            def _():
                for copy in stay_here():
                    copy.start()

    def all_of(ref, count, send_sem, recv_sem):
        rows = ref.at[0:count]
        return remote(rows, rows, send_sem, recv_sem, chip, core)

    def all_in(count):
        return all_of(held_means, count, mean_send, mean_recv), all_of(held, count * ROWS, in_send, in_recv)

    @pl.when(mine)
    def _():
        for copy in all_in(CHIPS - 1):
            copy.wait_recv()
        for copy in stay_here():
            copy.wait()

    @pl.when(not_mine)
    def _():
        for copy in all_in(CHIPS):
            copy.wait_recv()

    block_means = held_means[...]
    offsets = block_means - jnp.sum(block_means, axis=0, keepdims=True) / CHIPS
    centre = (held[...].astype(F32).reshape(CHIPS, ROWS, TILE) + offsets).reshape(SAMPLES, TILE)
    variance = jnp.sum(centre * centre, axis=0, keepdims=True) / SAMPLES
    inverse = lax.rsqrt(variance + eps_value)
    own[...] = (centre * inverse).astype(BF16)
    inv_own[...] = jnp.broadcast_to(inverse, inv_own.shape)
    swap = remote(own, other, pair_send.at[0], pair_recv.at[0], chip, 1 - core)
    swap_inv = remote(inv_own, inv_other, pair_send.at[1], pair_recv.at[1], chip, 1 - core)

    def step(phase, q, hop, src, dst):
        stride = ORDERS[q % 3][(0, 1, 2, 1, 0)[phase]]
        at = phase * CHAINS + q
        return remote(src, dst, ring_send.at[at], ring_recv.at[at], partner(chip, stride, hop), core)

    def first(q, hop):
        to = (coordinate(chip, ORDERS[q % 3][0]) + hop) % 4
        return step(0, q, hop, part.at[rows_at(q * PART + to * CHUNK, CHUNK), :], got_a.at[q, hop - 1])

    def second(q, hop):
        to = (coordinate(chip, ORDERS[q % 3][1]) + hop) % 4
        return step(1, q, hop, sum_a.at[q, rows_at(to * FINE, FINE), :], got_b.at[q, hop - 1])

    def third(q, hop):
        return step(2, q, hop, sum_b.at[q], got_c.at[q, hop - 1])

    def chunk_rows(q):
        return rows_at(q * PART + coordinate(chip, ORDERS[q % 3][0]) * CHUNK, CHUNK)

    def fine_rows(q):
        start = q * PART + coordinate(chip, ORDERS[q % 3][0]) * CHUNK + coordinate(chip, ORDERS[q % 3][1]) * FINE
        return rows_at(start, FINE)

    def fourth(q, hop):
        return step(3, q, hop, full.at[fine_rows(q), :], full.at[fine_rows(q), :])

    def fifth(q, hop):
        return step(4, q, hop, full.at[chunk_rows(q), :], full.at[chunk_rows(q), :])

    def chains(wave):
        return range(3 * wave, 3 * wave + 3)

    def start(phase, q):
        for hop in HOPS:
            phase(q, hop).start()

    def three(phase, q):
        at = phase * CHAINS + q
        all_three = (got_a, got_b, got_c, got_b, got_a)[phase].at[q]
        return remote(all_three, all_three, ring_send.at[at], ring_recv.at[at], chip, core)

    def arrived(phase, q):
        three(phase, q).wait_recv()

    def summed(mine_ref, got, q):
        total = mine_ref.astype(F32)
        for hop in HOPS:
            total = total + got[q, hop - 1].astype(F32)
        return total.astype(BF16)


    def sent_in():
        @pl.when(mine)
        def _():
            for copy in all_in(CHIPS - 1):
                copy.wait_send()

        @pl.when(not_mine)
        def _():
            for copy in all_in(CHIPS):
                copy.wait_send()

    swap.start()
    swap_inv.start()

    for wave in range(WAVES):
        blocks = list(enumerate(BLOCKS))[wave * 36 // WAVES:(wave + 1) * 36 // WAVES]
        for r in range(8):
            columns = [c for _, (row, c) in blocks if row == r]
            if columns:
                panel = lax.dot_general(
                    own[r * TILE:(r + 1) * TILE, :], own[columns[0] * TILE:(columns[-1] + 1) * TILE, :],
                    (((1,), (1,)), ((), ())), preferred_element_type=F32,
                )
                for at, (row, c) in blocks:
                    if row == r:
                        lanes = slice((c - columns[0]) * TILE, (c - columns[0] + 1) * TILE)
                        part[at * TILE:(at + 1) * TILE, :] = panel[:, lanes].astype(BF16)
        for q in chains(wave):
            start(first, q)

    sent_in()
    swap.wait()
    swap_inv.wait()
    scale_copy.wait()
    scale = scale_ref[0]
    corr = jnp.sum(own[...].astype(F32) * other[...].astype(F32), axis=0, keepdims=True) / SAMPLES
    diagonal = scale * (2.0 * (corr - 1.0) - 2.0 * offdiag_weight * corr)

    for wave in range(WAVES):
        for q in chains(wave):
            arrived(0, q)
            sum_a[q] = summed(part[chunk_rows(q), :], got_a, q)
            start(second, q)
    for wave in range(WAVES):
        for q in chains(wave):
            arrived(1, q)
            sum_b[q] = summed(sum_a[q, rows_at(coordinate(chip, ORDERS[q % 3][1]) * FINE, FINE), :], got_b, q)
            start(third, q)
    for wave in range(WAVES):
        for q in chains(wave):
            arrived(2, q)
            full[fine_rows(q), :] = summed(sum_b[q], got_c, q)
            start(fourth, q)
    for wave in range(WAVES):
        for q in chains(wave):
            arrived(3, q)
            start(fifth, q)

    for wave in range(WAVES):
        for q in chains(wave):
            arrived(4, q)
        for at, (r, c) in list(enumerate(BLOCKS))[wave * 36 // WAVES:(wave + 1) * 36 // WAVES]:
            block = full[at * TILE:(at + 1) * TILE, :]
            gram[r * TILE:(r + 1) * TILE, c * TILE:(c + 1) * TILE] = block
            if r != c:
                gram[c * TILE:(c + 1) * TILE, r * TILE:(r + 1) * TILE] = block.T
        since, until = WHOLE[wave], WHOLE[wave + 1]
        rows = jnp.dot(gram[since:until, since:], other[since:, :], preferred_element_type=F32)
        products[since:until, :] = rows if wave == 0 else products[since:until, :] + rows
        if until < SAMPLES:
            rest = jnp.dot(gram[until:, since:until], other[since:until, :], preferred_element_type=F32)
            products[until:, :] = rest if wave == 0 else products[until:, :] + rest
    theirs = other[...].astype(F32)
    back = products[...] * (scale * (2.0 * offdiag_weight / (SAMPLES * SAMPLES)))
    back = back + own[...].astype(F32) * (diagonal / SAMPLES)
    weight = jnp.sum(back * theirs, axis=0, keepdims=True) / SAMPLES
    grads[...] = (inv_other[0:1, :] * (back - theirs * weight)).astype(BF16)

    place = out.at[1 - core, :, lanes_at(tile)]

    def to_samples(chip_to):
        return remote(grads.at[rows_at(chip_to * ROWS, ROWS), :], place, out_send, out_recv, chip_to, half)

    for shift in SHIFTS[:-1]:
        to_samples(shifted(shift)).start()

    @pl.when(not_mine)
    def _():
        to_samples(chip).start()

    @pl.when(mine)
    def _():
        pltpu.make_async_copy(grads.at[rows_at(chip * ROWS, ROWS), :], place, local_sem.at[0]).start()

    for phase in range(PHASES):
        for q in range(CHAINS):
            three(phase, q).wait_send()

    @pl.when(mine)
    def _():
        all_of(grads, (CHIPS - 1) * ROWS, out_send, out_recv).wait()
        pltpu.make_async_copy(grads.at[rows_at(chip * ROWS, ROWS), :], place, local_sem.at[0]).wait()

    @pl.when(not_mine)
    def _():
        all_of(grads, CHIPS * ROWS, out_send, out_recv).wait()


def shards(view_one, view_two, loss_scale):
    hbm = pl.BlockSpec(memory_space=pltpu.HBM)
    out = pl.pallas_call(
        kernel,
        out_shape=jax.ShapeDtypeStruct((2, ROWS, WIDE), BF16),
        in_specs=[hbm, hbm, hbm],
        out_specs=pl.BlockSpec(memory_space=pltpu.VMEM),
        scratch_shapes=[
            pltpu.VMEM((2, ROWS, WIDE), F32),
            pltpu.VMEM((2, WIDE // TILE, 1, TILE), F32),
            pltpu.VMEM((2, ROWS, WIDE), BF16),
            pltpu.VMEM((SAMPLES, TILE), BF16),
            pltpu.VMEM((CHIPS, 1, TILE), F32),
            pltpu.VMEM((SAMPLES, TILE), BF16),
            pltpu.VMEM((SAMPLES, TILE), BF16),
            pltpu.VMEM((8, TILE), F32),
            pltpu.VMEM((8, TILE), F32),
            pltpu.VMEM((CHAINS * PART, TILE), BF16),
            pltpu.VMEM((CHAINS, 3, CHUNK, TILE), BF16),
            pltpu.VMEM((CHAINS, CHUNK, TILE), BF16),
            pltpu.VMEM((CHAINS, 3, FINE, TILE), BF16),
            pltpu.VMEM((CHAINS, FINE, TILE), BF16),
            pltpu.VMEM((CHAINS, 3, FINE, TILE), BF16),
            pltpu.VMEM((CHAINS * PART, TILE), BF16),
            pltpu.VMEM((SAMPLES, SAMPLES), BF16),
            pltpu.VMEM((SAMPLES, TILE), F32),
            pltpu.VMEM((SAMPLES, TILE), BF16),
            pltpu.SMEM((1,), F32),
            pltpu.SemaphoreType.DMA,
            pltpu.SemaphoreType.DMA,
            pltpu.SemaphoreType.DMA,
            pltpu.SemaphoreType.DMA,
            pltpu.SemaphoreType.DMA,
            pltpu.SemaphoreType.DMA,
            pltpu.SemaphoreType.DMA((2,)),
            pltpu.SemaphoreType.DMA((2,)),
            pltpu.SemaphoreType.DMA((PHASES * CHAINS,)),
            pltpu.SemaphoreType.DMA((PHASES * CHAINS,)),
            pltpu.SemaphoreType.DMA((2,)),
            pltpu.SemaphoreType.DMA((2,)),
            pltpu.SemaphoreType.DMA,
        ],
        compiler_params=pltpu.CompilerParams(
            collective_id=0, has_side_effects=True, vmem_limit_bytes=54848 * 1024
        ),
    )(view_one, view_two, loss_scale)
    return out[0].astype(F32), out[1].astype(F32)


def solution(mesh):
    placed = (P("dp", "feat"), P("dp", "feat"), P())
    return jax.shard_map(
        shards,
        mesh=mesh,
        in_specs=placed,
        out_specs=(P("dp", "feat"), P("dp", "feat")),
        check_vma=False,
    )
```

```python
import jax
import jax.numpy as jnp
from jax import lax
from jax.experimental import pallas as pl
from jax.experimental.pallas import tpu as pltpu
from jax.sharding import PartitionSpec as P

MESH = pl.DeviceIdType.MESH
F32, BF16 = jnp.float32, jnp.bfloat16

eps_value = 1e-05
offdiag_weight = 0.0051

CHIPS = 64
SAMPLES, ROWS, WIDE, TILE = 1024, 16, 4096, 128
BLOCKS = [(r, c) for r in range(8) for c in range(r, 8)]
WAVES = 3
CHAINS = 3 * WAVES
WHOLE = [0] + [min(r for r, c in BLOCKS[wave * 36 // WAVES:] + [(8, 8)]) * TILE for wave in range(1, WAVES + 1)]
PART = len(BLOCKS) * TILE // CHAINS
CHUNK, FINE = PART // 4, PART // 16
ORDERS = ((4, 16, 1), (16, 1, 4), (1, 4, 16))
HOPS = (2, 1, 3)
PHASES = 7


def apart(shift):
    return min(shift, 4 - shift)


SHIFTS = sorted(
    ((y, x, z) for y in range(4) for x in range(4) for z in range(4)), key=lambda s: -(apart(s[0]) + apart(s[1]) + apart(s[2]))
)
PLANE = [(x, z) for y, x, z in SHIFTS if y == 0]


def remote(src, dst, send_sem, recv_sem, chip, core):
    return pltpu.make_async_remote_copy(
        src_ref=src, dst_ref=dst, send_sem=send_sem, recv_sem=recv_sem, device_id=(chip, core), device_id_type=MESH
    )


def rows_at(start, size):
    return pl.ds(pl.multiple_of(start, 16), size)


def lanes_at(tile):
    return pl.ds(pl.multiple_of(tile * TILE, TILE), TILE)


def coordinate(chip, stride):
    return (chip // stride) % 4


def partner(chip, stride, hop):
    here = coordinate(chip, stride)
    return chip + ((here + hop) % 4 - here) * stride


def kernel(
    one, two, scale_hbm, out, views, means, rests, held, held_means, own, other, inv_own, inv_other, part, got_a, sum_a, got_b, sum_b, got_c, full, gram, products, grads,
    scale_ref, in_send, in_recv, mean_send, mean_recv, out_send, out_recv, pair_send, pair_recv, ring_send, ring_recv, local_sem, view_sem, scale_sem,
):
    chip, core = lax.axis_index("dp"), lax.axis_index("feat")
    half, tile = chip // 32, chip % 32
    mine = half == core
    not_mine = jnp.logical_not(mine)
    at_y, at_x, at_z = coordinate(chip, 16), coordinate(chip, 4), coordinate(chip, 1)

    def shifted(shift):
        y, x, z = shift
        return (at_y + y) % 4 * 16 + (at_x + x) % 4 * 4 + (at_z + z) % 4

    loads = [pltpu.make_async_copy(view, views.at[k], view_sem.at[k]) for k, view in enumerate((one, two))]
    for load in loads:
        load.start()

    barrier = pltpu.get_barrier_semaphore()
    for shift in SHIFTS[:-1]:
        pl.semaphore_signal(barrier, inc=1, device_id=(shifted(shift), half), device_id_type=MESH)

    @pl.when(not_mine)
    def _():
        pl.semaphore_signal(barrier, inc=1, device_id=(chip, half), device_id_type=MESH)

    scale_copy = pltpu.make_async_copy(scale_hbm, scale_ref, scale_sem)
    scale_copy.start()

    for k, load in enumerate(loads):
        load.wait()
        samples = views[k]
        block_mean = jnp.sum(samples, axis=0, keepdims=True) / ROWS
        rests[k] = (samples - block_mean).astype(BF16)
        for t in range(WIDE // TILE):
            means[k, t] = block_mean[:, t * TILE:(t + 1) * TILE]

    @pl.when(mine)
    def _():
        pl.semaphore_wait(barrier, CHIPS - 1)

    @pl.when(not_mine)
    def _():
        pl.semaphore_wait(barrier, CHIPS)

    my_rows = held.at[rows_at(chip * ROWS, ROWS), :]

    def to_owner(chip_to, core_to):
        t = chip_to % 32
        return (
            remote(means.at[core_to, t], held_means.at[chip], mean_send, mean_recv, chip_to, core_to),
            remote(rests.at[core_to, :, lanes_at(t)], my_rows, in_send, in_recv, chip_to, core_to),
        )

    def stay_here():
        return (
            pltpu.make_async_copy(means.at[core, tile], held_means.at[chip], local_sem.at[0]),
            pltpu.make_async_copy(rests.at[core, :, lanes_at(tile)], my_rows, local_sem.at[1]),
        )

    for x, z in PLANE[:-1]:
        for y in range(2):
            chip_to = (2 * core + y) * 16 + (at_x + x) % 4 * 4 + (at_z + z) % 4
            for core_to in range(2):
                for copy in to_owner(chip_to, core_to):
                    copy.start()
    for y in range(2):
        chip_to = (2 * core + y) * 16 + at_x * 4 + at_z
        for core_to in range(2):
            stays = jnp.logical_and(chip_to == chip, core == core_to)

            @pl.when(jnp.logical_not(stays))
            def _():
                for copy in to_owner(chip_to, core_to):
                    copy.start()

            @pl.when(stays)
            def _():
                for copy in stay_here():
                    copy.start()

    def all_of(ref, count, send_sem, recv_sem):
        rows = ref.at[0:count]
        return remote(rows, rows, send_sem, recv_sem, chip, core)

    def all_in(count):
        return all_of(held_means, count, mean_send, mean_recv), all_of(held, count * ROWS, in_send, in_recv)

    @pl.when(mine)
    def _():
        for copy in all_in(CHIPS - 1):
            copy.wait_recv()
        for copy in stay_here():
            copy.wait()

    @pl.when(not_mine)
    def _():
        for copy in all_in(CHIPS):
            copy.wait_recv()

    block_means = held_means[...]
    offsets = block_means - jnp.sum(block_means, axis=0, keepdims=True) / CHIPS
    centre = (held[...].astype(F32).reshape(CHIPS, ROWS, TILE) + offsets).reshape(SAMPLES, TILE)
    variance = jnp.sum(centre * centre, axis=0, keepdims=True) / SAMPLES
    inverse = lax.rsqrt(variance + eps_value)
    own[...] = (centre * inverse).astype(BF16)
    inv_own[...] = jnp.broadcast_to(inverse, inv_own.shape)
    swap = remote(own, other, pair_send.at[0], pair_recv.at[0], chip, 1 - core)
    swap_inv = remote(inv_own, inv_other, pair_send.at[1], pair_recv.at[1], chip, 1 - core)

    def step(phase, q, hop, src, dst):
        stride = ORDERS[q % 3][(0, 1, 2, 1, 0, 0, 0)[phase]]
        at = phase * CHAINS + q
        return remote(src, dst, ring_send.at[at], ring_recv.at[at], partner(chip, stride, hop), core)

    def piece_rows(at, piece):
        turn = coordinate(chip, ORDERS[at // 4 % 3][1])
        return rows_at(at * TILE + (piece - turn + 4) % 4 * FINE, FINE)

    def chunk_start(q, hop=0):
        return q * PART + (coordinate(chip, ORDERS[q % 3][0]) + hop) % 4 * CHUNK

    def own_rows(q, hop=0):
        return rows_at(chunk_start(q, hop), FINE)

    def further_rows(q, hop=0):
        return rows_at(chunk_start(q, hop) + FINE, 3 * FINE)

    def first(q, hop):
        return step(0, q, hop, part.at[further_rows(q, hop), :], got_a.at[q, hop - 1, FINE:CHUNK])

    def first_own(q, hop):
        return step(5, q, hop, part.at[own_rows(q, hop), :], got_a.at[q, hop - 1, 0:FINE])

    def second(q, hop):
        return step(1, q, hop, sum_a.at[q, hop * FINE:(hop + 1) * FINE, :], got_b.at[q, hop - 1])

    def third(q, hop):
        return step(2, q, hop, sum_b.at[q], got_c.at[q, hop - 1])

    def fourth(q, hop):
        landing = rows_at(chunk_start(q) + (4 - hop) * FINE, FINE)
        return step(3, q, hop, full.at[own_rows(q), :], full.at[landing, :])

    def fourth_own(q, hop):
        return step(6, q, hop, full.at[own_rows(q), :], full.at[own_rows(q), :])

    def fifth(q, hop):
        return step(4, q, hop, full.at[further_rows(q), :], full.at[further_rows(q), :])

    def chains(wave):
        return range(3 * wave, 3 * wave + 3)

    def start(phase, q):
        for hop in HOPS:
            phase(q, hop).start()

    def three(phase, q):
        at = phase * CHAINS + q
        all_three = part.at[0:9 * FINE, :] if phase in (0, 4) else got_b.at[q]
        return remote(all_three, all_three, ring_send.at[at], ring_recv.at[at], chip, core)

    def arrived(phase, q):
        three(phase, q).wait_recv()

    def summed(*terms):
        total = terms[0].astype(F32)
        for term in terms[1:]:
            total = total + term.astype(F32)
        return total.astype(BF16)


    def sent_in():
        @pl.when(mine)
        def _():
            for copy in all_in(CHIPS - 1):
                copy.wait_send()

        @pl.when(not_mine)
        def _():
            for copy in all_in(CHIPS):
                copy.wait_send()

    swap.start()
    swap_inv.start()

    for wave in range(WAVES):
        blocks = list(enumerate(BLOCKS))[wave * 36 // WAVES:(wave + 1) * 36 // WAVES]
        for r in range(8):
            columns = [c for _, (row, c) in blocks if row == r]
            if columns:
                panel = lax.dot_general(
                    own[r * TILE:(r + 1) * TILE, :], own[columns[0] * TILE:(columns[-1] + 1) * TILE, :],
                    (((1,), (1,)), ((), ())), preferred_element_type=F32,
                )
                for at, (row, c) in blocks:
                    if row == r:
                        block = panel[:, (c - columns[0]) * TILE:(c - columns[0] + 1) * TILE].astype(BF16)
                        for k in range(4):
                            part[piece_rows(at, k), :] = block[k * FINE:(k + 1) * FINE, :]
        for q in chains(wave):
            start(first, q)
    for q in range(CHAINS):
        start(first_own, q)

    sent_in()
    swap.wait()
    swap_inv.wait()
    scale_copy.wait()
    scale = scale_ref[0]
    corr = jnp.sum(own[...].astype(F32) * other[...].astype(F32), axis=0, keepdims=True) / SAMPLES
    diagonal = scale * (2.0 * (corr - 1.0) - 2.0 * offdiag_weight * corr)

    for q in range(CHAINS):
        arrived(0, q)
        further = slice(FINE, CHUNK)
        sum_a[q, further] = summed(part[further_rows(q), :], *(got_a[q, k, further] for k in range(3)))
        start(second, q)
    for q in range(CHAINS):
        arrived(5, q)
        arrived(1, q)
        sum_b[q] = summed(part[own_rows(q), :], *(got_a[q, k, 0:FINE] for k in range(3)), *(got_b[q, k] for k in range(3)))
        start(third, q)
    for q in range(CHAINS):
        arrived(2, q)
        full[own_rows(q), :] = summed(sum_b[q], *(got_c[q, k] for k in range(3)))
        start(fourth, q)
        start(fourth_own, q)
    for q in range(CHAINS):
        arrived(3, q)
        start(fifth, q)

    for wave in range(WAVES):
        for q in chains(wave):
            arrived(6, q)
            arrived(4, q)
        for at, (r, c) in list(enumerate(BLOCKS))[wave * 36 // WAVES:(wave + 1) * 36 // WAVES]:
            block = jnp.concatenate([full[piece_rows(at, k), :] for k in range(4)], axis=0)
            gram[r * TILE:(r + 1) * TILE, c * TILE:(c + 1) * TILE] = block
            if r != c:
                gram[c * TILE:(c + 1) * TILE, r * TILE:(r + 1) * TILE] = block.T
        since, until = WHOLE[wave], WHOLE[wave + 1]
        rows = jnp.dot(gram[since:until, since:], other[since:, :], preferred_element_type=F32)
        products[since:until, :] = rows if wave == 0 else products[since:until, :] + rows
        if until < SAMPLES:
            rest = jnp.dot(gram[until:, since:until], other[since:until, :], preferred_element_type=F32)
            products[until:, :] = rest if wave == 0 else products[until:, :] + rest
    theirs = other[...].astype(F32)
    back = products[...] * (scale * (2.0 * offdiag_weight / (SAMPLES * SAMPLES)))
    back = back + own[...].astype(F32) * (diagonal / SAMPLES)
    weight = jnp.sum(back * theirs, axis=0, keepdims=True) / SAMPLES
    grads[...] = (inv_other[0:1, :] * (back - theirs * weight)).astype(BF16)

    place = out.at[1 - core, :, lanes_at(tile)]

    def to_samples(chip_to):
        return remote(grads.at[rows_at(chip_to * ROWS, ROWS), :], place, out_send, out_recv, chip_to, half)

    for y in range(4):
        for x, z in PLANE[:-1]:
            to_samples(y * 16 + (at_x + x) % 4 * 4 + (at_z + z) % 4).start()
    for dy in (2, 1, 3):
        to_samples(shifted((dy, 0, 0))).start()

    @pl.when(not_mine)
    def _():
        to_samples(chip).start()

    @pl.when(mine)
    def _():
        pltpu.make_async_copy(grads.at[rows_at(chip * ROWS, ROWS), :], place, local_sem.at[0]).start()

    for phase in range(PHASES):
        for q in range(CHAINS):
            three(phase, q).wait_send()

    @pl.when(mine)
    def _():
        all_of(grads, (CHIPS - 1) * ROWS, out_send, out_recv).wait()
        pltpu.make_async_copy(grads.at[rows_at(chip * ROWS, ROWS), :], place, local_sem.at[0]).wait()

    @pl.when(not_mine)
    def _():
        all_of(grads, CHIPS * ROWS, out_send, out_recv).wait()


def shards(view_one, view_two, loss_scale):
    hbm = pl.BlockSpec(memory_space=pltpu.HBM)
    out = pl.pallas_call(
        kernel,
        out_shape=jax.ShapeDtypeStruct((2, ROWS, WIDE), BF16),
        in_specs=[hbm, hbm, hbm],
        out_specs=pl.BlockSpec(memory_space=pltpu.VMEM),
        scratch_shapes=[
            pltpu.VMEM((2, ROWS, WIDE), F32),
            pltpu.VMEM((2, WIDE // TILE, 1, TILE), F32),
            pltpu.VMEM((2, ROWS, WIDE), BF16),
            pltpu.VMEM((SAMPLES, TILE), BF16),
            pltpu.VMEM((CHIPS, 1, TILE), F32),
            pltpu.VMEM((SAMPLES, TILE), BF16),
            pltpu.VMEM((SAMPLES, TILE), BF16),
            pltpu.VMEM((8, TILE), F32),
            pltpu.VMEM((8, TILE), F32),
            pltpu.VMEM((CHAINS * PART, TILE), BF16),
            pltpu.VMEM((CHAINS, 3, CHUNK, TILE), BF16),
            pltpu.VMEM((CHAINS, CHUNK, TILE), BF16),
            pltpu.VMEM((CHAINS, 3, FINE, TILE), BF16),
            pltpu.VMEM((CHAINS, FINE, TILE), BF16),
            pltpu.VMEM((CHAINS, 3, FINE, TILE), BF16),
            pltpu.VMEM((CHAINS * PART, TILE), BF16),
            pltpu.VMEM((SAMPLES, SAMPLES), BF16),
            pltpu.VMEM((SAMPLES, TILE), F32),
            pltpu.VMEM((SAMPLES, TILE), BF16),
            pltpu.SMEM((1,), F32),
            pltpu.SemaphoreType.DMA,
            pltpu.SemaphoreType.DMA,
            pltpu.SemaphoreType.DMA,
            pltpu.SemaphoreType.DMA,
            pltpu.SemaphoreType.DMA,
            pltpu.SemaphoreType.DMA,
            pltpu.SemaphoreType.DMA((2,)),
            pltpu.SemaphoreType.DMA((2,)),
            pltpu.SemaphoreType.DMA((PHASES * CHAINS,)),
            pltpu.SemaphoreType.DMA((PHASES * CHAINS,)),
            pltpu.SemaphoreType.DMA((2,)),
            pltpu.SemaphoreType.DMA((2,)),
            pltpu.SemaphoreType.DMA,
        ],
        compiler_params=pltpu.CompilerParams(
            collective_id=0, has_side_effects=True, vmem_limit_bytes=54848 * 1024
        ),
    )(view_one, view_two, loss_scale)
    return out[0].astype(F32), out[1].astype(F32)


def solution(mesh):
    placed = (P("dp", "feat"), P("dp", "feat"), P())
    return jax.shard_map(
        shards,
        mesh=mesh,
        in_specs=placed,
        out_specs=(P("dp", "feat"), P("dp", "feat")),
        check_vma=False,
    )
```

```python
import jax
import jax.numpy as jnp
from jax import lax
from jax.experimental import pallas as pl
from jax.experimental.pallas import tpu as pltpu
from jax.sharding import PartitionSpec as P

MESH = pl.DeviceIdType.MESH
F32, BF16 = jnp.float32, jnp.bfloat16

eps_value = 1e-05
offdiag_weight = 0.0051

CHIPS = 64
SAMPLES, ROWS, WIDE, TILE = 1024, 16, 4096, 128
BLOCKS = [(r, c) for r in range(8) for c in range(r, 8)]
WAVES = 3
CHAINS = 3 * WAVES
WHOLE = [0] + [min(r for r, c in BLOCKS[wave * 36 // WAVES:] + [(8, 8)]) * TILE for wave in range(1, WAVES + 1)]
PART = len(BLOCKS) * TILE // CHAINS
CHUNK, FINE = PART // 4, PART // 16
ORDERS = ((4, 16, 1), (16, 1, 4), (1, 4, 16))
HOPS = (2, 1, 3)
PHASES = 5


def apart(shift):
    return min(shift, 4 - shift)


SHIFTS = sorted(
    ((y, x, z) for y in range(4) for x in range(4) for z in range(4)), key=lambda s: -(apart(s[0]) + apart(s[1]) + apart(s[2]))
)
PLANE = [(x, z) for y, x, z in SHIFTS if y == 0]


def remote(src, dst, send_sem, recv_sem, chip, core):
    return pltpu.make_async_remote_copy(
        src_ref=src, dst_ref=dst, send_sem=send_sem, recv_sem=recv_sem, device_id=(chip, core), device_id_type=MESH
    )


def rows_at(start, size):
    return pl.ds(pl.multiple_of(start, 16), size)


def lanes_at(tile):
    return pl.ds(pl.multiple_of(tile * TILE, TILE), TILE)


def coordinate(chip, stride):
    return (chip // stride) % 4


def partner(chip, stride, hop):
    here = coordinate(chip, stride)
    return chip + ((here + hop) % 4 - here) * stride


def kernel(
    one, two, scale_hbm, out, views, means, rests, held, held_means, own, other, inv_own, inv_other, part, got_a, sum_a, got_b, sum_b, got_c, full, gram, products, grads,
    scale_ref, in_send, in_recv, mean_send, mean_recv, out_send, out_recv, pair_send, pair_recv, ring_send, ring_recv, local_sem, view_sem, scale_sem,
):
    chip, core = lax.axis_index("dp"), lax.axis_index("feat")
    half, tile = chip // 32, chip % 32
    mine = half == core
    not_mine = jnp.logical_not(mine)
    at_y, at_x, at_z = coordinate(chip, 16), coordinate(chip, 4), coordinate(chip, 1)

    def shifted(shift):
        y, x, z = shift
        return (at_y + y) % 4 * 16 + (at_x + x) % 4 * 4 + (at_z + z) % 4

    loads = [pltpu.make_async_copy(view, views.at[k], view_sem.at[k]) for k, view in enumerate((one, two))]
    for load in loads:
        load.start()

    barrier = pltpu.get_barrier_semaphore()
    for shift in SHIFTS[:-1]:
        pl.semaphore_signal(barrier, inc=1, device_id=(shifted(shift), half), device_id_type=MESH)

    @pl.when(not_mine)
    def _():
        pl.semaphore_signal(barrier, inc=1, device_id=(chip, half), device_id_type=MESH)

    scale_copy = pltpu.make_async_copy(scale_hbm, scale_ref, scale_sem)
    scale_copy.start()

    for k, load in enumerate(loads):
        load.wait()
        samples = views[k]
        block_mean = jnp.sum(samples, axis=0, keepdims=True) / ROWS
        rest = (samples - block_mean).astype(BF16)
        for t in range(WIDE // TILE):
            means[k, t] = block_mean[:, t * TILE:(t + 1) * TILE]
            rests[k, t] = rest[:, t * TILE:(t + 1) * TILE]

    @pl.when(mine)
    def _():
        pl.semaphore_wait(barrier, CHIPS - 1)

    @pl.when(not_mine)
    def _():
        pl.semaphore_wait(barrier, CHIPS)

    my_rows = held.at[rows_at(chip * ROWS, ROWS), :]

    def to_owner(chip_to, core_to):
        t = chip_to % 32
        return (
            remote(means.at[core_to, t], held_means.at[chip], mean_send, mean_recv, chip_to, core_to),
            remote(rests.at[core_to, t], my_rows, in_send, in_recv, chip_to, core_to),
        )

    def stay_here():
        return (
            pltpu.make_async_copy(means.at[core, tile], held_means.at[chip], local_sem.at[0]),
            pltpu.make_async_copy(rests.at[core, tile], my_rows, local_sem.at[1]),
        )

    for x, z in PLANE[:-1]:
        for y in range(2):
            chip_to = (2 * core + y) * 16 + (at_x + x) % 4 * 4 + (at_z + z) % 4
            for core_to in range(2):
                for copy in to_owner(chip_to, core_to):
                    copy.start()
    for y in range(2):
        chip_to = (2 * core + y) * 16 + at_x * 4 + at_z
        for core_to in range(2):
            stays = jnp.logical_and(chip_to == chip, core == core_to)

            @pl.when(jnp.logical_not(stays))
            def _():
                for copy in to_owner(chip_to, core_to):
                    copy.start()

            @pl.when(stays)
            def _():
                for copy in stay_here():
                    copy.start()

    def all_of(ref, count, send_sem, recv_sem):
        rows = ref.at[0:count]
        return remote(rows, rows, send_sem, recv_sem, chip, core)

    def all_in(count):
        return all_of(held_means, count, mean_send, mean_recv), all_of(held, count * ROWS, in_send, in_recv)

    @pl.when(mine)
    def _():
        for copy in all_in(CHIPS - 1):
            copy.wait_recv()
        for copy in stay_here():
            copy.wait()

    @pl.when(not_mine)
    def _():
        for copy in all_in(CHIPS):
            copy.wait_recv()

    block_means = held_means[...]
    offsets = block_means - jnp.sum(block_means, axis=0, keepdims=True) / CHIPS
    centre = (held[...].astype(F32).reshape(CHIPS, ROWS, TILE) + offsets).reshape(SAMPLES, TILE)
    variance = jnp.sum(centre * centre, axis=0, keepdims=True) / SAMPLES
    inverse = lax.rsqrt(variance + eps_value)
    own[...] = (centre * inverse).astype(BF16)
    inv_own[...] = jnp.broadcast_to(inverse, inv_own.shape)
    swap = remote(own, other, pair_send.at[0], pair_recv.at[0], chip, 1 - core)
    swap_inv = remote(inv_own, inv_other, pair_send.at[1], pair_recv.at[1], chip, 1 - core)

    def step(phase, q, hop, src, dst):
        stride = ORDERS[q % 3][(0, 1, 2, 1, 0, 0, 0)[phase]]
        at = (0, 1, 2, 3, 4, 1, 4)[phase] * CHAINS + q
        return remote(src, dst, ring_send.at[q], ring_recv.at[at], partner(chip, stride, hop), core)

    def piece_rows(at, piece):
        turn = coordinate(chip, ORDERS[at // 4 % 3][1])
        return rows_at(at * TILE + (piece - turn + 4) % 4 * FINE, FINE)

    def chunk_start(q, hop=0):
        return q * PART + (coordinate(chip, ORDERS[q % 3][0]) + hop) % 4 * CHUNK

    def own_rows(q, hop=0):
        return rows_at(chunk_start(q, hop), FINE)

    def further_rows(q, hop=0):
        return rows_at(chunk_start(q, hop) + FINE, 3 * FINE)

    def first(q, hop):
        return step(0, q, hop, part.at[further_rows(q, hop), :], got_a.at[q, hop - 1, FINE:CHUNK])

    def first_own(q, hop):
        return step(5, q, hop, part.at[own_rows(q, hop), :], got_a.at[q, hop - 1, 0:FINE])

    def second(q, hop):
        return step(1, q, hop, sum_a.at[q, hop * FINE:(hop + 1) * FINE, :], got_b.at[q, hop - 1])

    def third(q, hop):
        return step(2, q, hop, sum_b.at[q], got_c.at[q, hop - 1])

    def fourth(q, hop):
        landing = rows_at(chunk_start(q) + (4 - hop) * FINE, FINE)
        return step(3, q, hop, full.at[own_rows(q), :], full.at[landing, :])

    def fourth_own(q, hop):
        return step(6, q, hop, full.at[own_rows(q), :], full.at[own_rows(q), :])

    def fifth(q, hop):
        return step(4, q, hop, full.at[further_rows(q), :], full.at[further_rows(q), :])

    def chains(wave):
        return range(3 * wave, 3 * wave + 3)

    def start(phase, q):
        for hop in HOPS:
            phase(q, hop).start()

    def waits(phase, q, pieces):
        rows = part.at[0:pieces * FINE, :]
        return remote(rows, rows, ring_send.at[q], ring_recv.at[phase * CHAINS + q], chip, core)

    def arrived(phase, q):
        waits(phase, q, (9, 6, 3, 3, 12)[phase]).wait_recv()

    def summed(*terms):
        total = terms[0].astype(F32)
        for term in terms[1:]:
            total = total + term.astype(F32)
        return total.astype(BF16)


    def sent_in():
        @pl.when(mine)
        def _():
            for copy in all_in(CHIPS - 1):
                copy.wait_send()

        @pl.when(not_mine)
        def _():
            for copy in all_in(CHIPS):
                copy.wait_send()

    swap.start()
    swap_inv.start()

    for wave in range(WAVES):
        blocks = list(enumerate(BLOCKS))[wave * 36 // WAVES:(wave + 1) * 36 // WAVES]
        for r in range(8):
            columns = [c for _, (row, c) in blocks if row == r]
            if columns:
                panel = lax.dot_general(
                    own[r * TILE:(r + 1) * TILE, :], own[columns[0] * TILE:(columns[-1] + 1) * TILE, :],
                    (((1,), (1,)), ((), ())), preferred_element_type=F32,
                )
                for at, (row, c) in blocks:
                    if row == r:
                        block = panel[:, (c - columns[0]) * TILE:(c - columns[0] + 1) * TILE].astype(BF16)
                        for k in range(4):
                            part[piece_rows(at, k), :] = block[k * FINE:(k + 1) * FINE, :]
        for q in chains(wave):
            start(first, q)
    for q in range(CHAINS):
        start(first_own, q)

    sent_in()
    swap.wait()
    swap_inv.wait()
    scale_copy.wait()
    scale = scale_ref[0]
    corr = jnp.sum(own[...].astype(F32) * other[...].astype(F32), axis=0, keepdims=True) / SAMPLES
    diagonal = scale * (2.0 * (corr - 1.0) - 2.0 * offdiag_weight * corr)

    for q in range(CHAINS):
        arrived(0, q)
        further = slice(FINE, CHUNK)
        sum_a[q, further] = summed(part[further_rows(q), :], *(got_a[q, k, further] for k in range(3)))
        start(second, q)
    for q in range(CHAINS):
        arrived(1, q)
        sum_b[q] = summed(part[own_rows(q), :], *(got_a[q, k, 0:FINE] for k in range(3)), *(got_b[q, k] for k in range(3)))
        start(third, q)
    for q in range(CHAINS):
        arrived(2, q)
        full[own_rows(q), :] = summed(sum_b[q], *(got_c[q, k] for k in range(3)))
        start(fourth, q)
        start(fourth_own, q)
    for q in range(CHAINS):
        arrived(3, q)
        start(fifth, q)

    for wave in range(WAVES):
        for q in chains(wave):
            arrived(4, q)
        for at, (r, c) in list(enumerate(BLOCKS))[wave * 36 // WAVES:(wave + 1) * 36 // WAVES]:
            block = jnp.concatenate([full[piece_rows(at, k), :] for k in range(4)], axis=0)
            gram[r * TILE:(r + 1) * TILE, c * TILE:(c + 1) * TILE] = block
            if r != c:
                gram[c * TILE:(c + 1) * TILE, r * TILE:(r + 1) * TILE] = block.T
        since, until = WHOLE[wave], WHOLE[wave + 1]
        rows = jnp.dot(gram[since:until, since:], other[since:, :], preferred_element_type=F32)
        products[since:until, :] = rows if wave == 0 else products[since:until, :] + rows
        if until < SAMPLES:
            rest = jnp.dot(gram[until:, since:until], other[since:until, :], preferred_element_type=F32)
            products[until:, :] = rest if wave == 0 else products[until:, :] + rest
    theirs = other[...].astype(F32)
    back = products[...] * (scale * (2.0 * offdiag_weight / (SAMPLES * SAMPLES)))
    back = back + own[...].astype(F32) * (diagonal / SAMPLES)
    weight = jnp.sum(back * theirs, axis=0, keepdims=True) / SAMPLES
    grads[...] = (inv_other[0:1, :] * (back - theirs * weight)).astype(BF16)

    place = out.at[1 - core, :, lanes_at(tile)]

    def to_samples(chip_to):
        return remote(grads.at[rows_at(chip_to * ROWS, ROWS), :], place, out_send, out_recv, chip_to, half)

    for y in range(4):
        for x, z in PLANE[:-1]:
            to_samples(y * 16 + (at_x + x) % 4 * 4 + (at_z + z) % 4).start()
    for dy in (2, 1, 3):
        to_samples(shifted((dy, 0, 0))).start()

    @pl.when(not_mine)
    def _():
        to_samples(chip).start()

    @pl.when(mine)
    def _():
        pltpu.make_async_copy(grads.at[rows_at(chip * ROWS, ROWS), :], place, local_sem.at[0]).start()

    for q in range(CHAINS):
        waits(0, q, 33).wait_send()

    @pl.when(mine)
    def _():
        all_of(grads, (CHIPS - 1) * ROWS, out_send, out_recv).wait()
        pltpu.make_async_copy(grads.at[rows_at(chip * ROWS, ROWS), :], place, local_sem.at[0]).wait()

    @pl.when(not_mine)
    def _():
        all_of(grads, CHIPS * ROWS, out_send, out_recv).wait()


def shards(view_one, view_two, loss_scale):
    hbm = pl.BlockSpec(memory_space=pltpu.HBM)
    out = pl.pallas_call(
        kernel,
        out_shape=jax.ShapeDtypeStruct((2, ROWS, WIDE), BF16),
        in_specs=[hbm, hbm, hbm],
        out_specs=pl.BlockSpec(memory_space=pltpu.VMEM),
        scratch_shapes=[
            pltpu.VMEM((2, ROWS, WIDE), F32),
            pltpu.VMEM((2, WIDE // TILE, 1, TILE), F32),
            pltpu.VMEM((2, WIDE // TILE, ROWS, TILE), BF16),
            pltpu.VMEM((SAMPLES, TILE), BF16),
            pltpu.VMEM((CHIPS, 1, TILE), F32),
            pltpu.VMEM((SAMPLES, TILE), BF16),
            pltpu.VMEM((SAMPLES, TILE), BF16),
            pltpu.VMEM((8, TILE), F32),
            pltpu.VMEM((8, TILE), F32),
            pltpu.VMEM((CHAINS * PART, TILE), BF16),
            pltpu.VMEM((CHAINS, 3, CHUNK, TILE), BF16),
            pltpu.VMEM((CHAINS, CHUNK, TILE), BF16),
            pltpu.VMEM((CHAINS, 3, FINE, TILE), BF16),
            pltpu.VMEM((CHAINS, FINE, TILE), BF16),
            pltpu.VMEM((CHAINS, 3, FINE, TILE), BF16),
            pltpu.VMEM((CHAINS * PART, TILE), BF16),
            pltpu.VMEM((SAMPLES, SAMPLES), BF16),
            pltpu.VMEM((SAMPLES, TILE), F32),
            pltpu.VMEM((SAMPLES, TILE), BF16),
            pltpu.SMEM((1,), F32),
            pltpu.SemaphoreType.DMA,
            pltpu.SemaphoreType.DMA,
            pltpu.SemaphoreType.DMA,
            pltpu.SemaphoreType.DMA,
            pltpu.SemaphoreType.DMA,
            pltpu.SemaphoreType.DMA,
            pltpu.SemaphoreType.DMA((2,)),
            pltpu.SemaphoreType.DMA((2,)),
            pltpu.SemaphoreType.DMA((CHAINS,)),
            pltpu.SemaphoreType.DMA((PHASES * CHAINS,)),
            pltpu.SemaphoreType.DMA((2,)),
            pltpu.SemaphoreType.DMA((2,)),
            pltpu.SemaphoreType.DMA,
        ],
        compiler_params=pltpu.CompilerParams(
            collective_id=0, has_side_effects=True, vmem_limit_bytes=54848 * 1024
        ),
    )(view_one, view_two, loss_scale)
    return out[0].astype(F32), out[1].astype(F32)


def solution(mesh):
    placed = (P("dp", "feat"), P("dp", "feat"), P())
    return jax.shard_map(
        shards,
        mesh=mesh,
        in_specs=placed,
        out_specs=(P("dp", "feat"), P("dp", "feat")),
        check_vma=False,
    )
```

```python
import jax
import jax.numpy as jnp
from jax import lax
from jax.experimental import pallas as pl
from jax.experimental.pallas import tpu as pltpu
from jax.sharding import PartitionSpec as P

MESH = pl.DeviceIdType.MESH
F32, BF16 = jnp.float32, jnp.bfloat16

eps_value = 1e-05
offdiag_weight = 0.0051

CHIPS = 64
SAMPLES, ROWS, WIDE, TILE = 1024, 16, 4096, 128
BLOCKS = [(r, c) for r in range(8) for c in range(r, 8)]
WAVES = 3
CHAINS = 3 * WAVES
WHOLE = [0] + [min(r for r, c in BLOCKS[wave * 36 // WAVES:] + [(8, 8)]) * TILE for wave in range(1, WAVES + 1)]
PART = len(BLOCKS) * TILE // CHAINS
CHUNK, FINE = PART // 4, PART // 16
ORDERS = ((4, 16, 1), (16, 1, 4), (1, 4, 16))
HOPS = (2, 1, 3)
PHASES = 5


def apart(shift):
    return min(shift, 4 - shift)


SHIFTS = sorted(
    ((y, x, z) for y in range(4) for x in range(4) for z in range(4)), key=lambda s: -(apart(s[0]) + apart(s[1]) + apart(s[2]))
)
PLANE = [(x, z) for y, x, z in SHIFTS if y == 0]


def remote(src, dst, send_sem, recv_sem, chip, core):
    return pltpu.make_async_remote_copy(
        src_ref=src, dst_ref=dst, send_sem=send_sem, recv_sem=recv_sem, device_id=(chip, core), device_id_type=MESH
    )


def rows_at(start, size):
    return pl.ds(pl.multiple_of(start, 16), size)


def lanes_at(tile):
    return pl.ds(pl.multiple_of(tile * TILE, TILE), TILE)


def coordinate(chip, stride):
    return (chip // stride) % 4


def partner(chip, stride, hop):
    here = coordinate(chip, stride)
    return chip + ((here + hop) % 4 - here) * stride


def kernel(
    one, two, scale_hbm, out, views, means, rests, held, held_means, own, other, inv_own, inv_other, part, got_a, sum_a, got_b, sum_b, got_c, full, gram, products, grads,
    scale_ref, in_send, in_recv, mean_send, mean_recv, out_send, out_recv, pair_send, pair_recv, ring_send, ring_recv, local_sem, view_sem, scale_sem,
):
    chip, core = lax.axis_index("dp"), lax.axis_index("feat")
    half, tile = chip // 32, chip % 32
    mine = half == core
    not_mine = jnp.logical_not(mine)
    at_y, at_x, at_z = coordinate(chip, 16), coordinate(chip, 4), coordinate(chip, 1)

    def shifted(shift):
        y, x, z = shift
        return (at_y + y) % 4 * 16 + (at_x + x) % 4 * 4 + (at_z + z) % 4

    loads = [pltpu.make_async_copy(view, views.at[k], view_sem.at[k]) for k, view in enumerate((one, two))]
    for load in loads:
        load.start()

    barrier = pltpu.get_barrier_semaphore()
    for shift in SHIFTS[:-1]:
        pl.semaphore_signal(barrier, inc=1, device_id=(shifted(shift), half), device_id_type=MESH)

    @pl.when(not_mine)
    def _():
        pl.semaphore_signal(barrier, inc=1, device_id=(chip, half), device_id_type=MESH)

    scale_copy = pltpu.make_async_copy(scale_hbm, scale_ref, scale_sem)
    scale_copy.start()

    for k, load in enumerate(loads):
        load.wait()
        samples = views[k]
        block_mean = jnp.sum(samples, axis=0, keepdims=True) / ROWS
        rest = (samples - block_mean).astype(BF16)
        for t in range(WIDE // TILE):
            means[k, t] = block_mean[:, t * TILE:(t + 1) * TILE]
            rests[k, t] = rest[:, t * TILE:(t + 1) * TILE]

    @pl.when(mine)
    def _():
        pl.semaphore_wait(barrier, CHIPS - 1)

    @pl.when(not_mine)
    def _():
        pl.semaphore_wait(barrier, CHIPS)

    my_rows = held.at[rows_at(chip * ROWS, ROWS), :]

    def to_owner(chip_to, core_to):
        t = chip_to % 32
        return (
            remote(means.at[core_to, t], held_means.at[chip], mean_send, mean_recv, chip_to, core_to),
            remote(rests.at[core_to, t], my_rows, in_send, in_recv, chip_to, core_to),
        )

    def stay_here():
        return (
            pltpu.make_async_copy(means.at[core, tile], held_means.at[chip], local_sem.at[0]),
            pltpu.make_async_copy(rests.at[core, tile], my_rows, local_sem.at[1]),
        )

    for x, z in PLANE[:-1]:
        for y in range(2):
            chip_to = (2 * core + y) * 16 + (at_x + x) % 4 * 4 + (at_z + z) % 4
            for core_to in range(2):
                for copy in to_owner(chip_to, core_to):
                    copy.start()
    for y in range(2):
        chip_to = (2 * core + y) * 16 + at_x * 4 + at_z
        for core_to in range(2):
            stays = jnp.logical_and(chip_to == chip, core == core_to)

            @pl.when(jnp.logical_not(stays))
            def _():
                for copy in to_owner(chip_to, core_to):
                    copy.start()

            @pl.when(stays)
            def _():
                for copy in stay_here():
                    copy.start()

    def all_of(ref, count, send_sem, recv_sem):
        rows = ref.at[0:count]
        return remote(rows, rows, send_sem, recv_sem, chip, core)

    def all_in(count):
        return all_of(held_means, count, mean_send, mean_recv), all_of(held, count * ROWS, in_send, in_recv)

    @pl.when(mine)
    def _():
        for copy in all_in(CHIPS - 1):
            copy.wait_recv()
        for copy in stay_here():
            copy.wait()

    @pl.when(not_mine)
    def _():
        for copy in all_in(CHIPS):
            copy.wait_recv()

    block_means = held_means[...]
    offsets = block_means - jnp.sum(block_means, axis=0, keepdims=True) / CHIPS
    centre = (held[...].astype(F32).reshape(CHIPS, ROWS, TILE) + offsets).reshape(SAMPLES, TILE)
    variance = jnp.sum(centre * centre, axis=0, keepdims=True) / SAMPLES
    inverse = lax.rsqrt(variance + eps_value)
    own[...] = (centre * inverse).astype(BF16)
    inv_own[...] = jnp.broadcast_to(inverse, inv_own.shape)
    swap = remote(own, other, pair_send.at[0], pair_recv.at[0], chip, 1 - core)
    swap_inv = remote(inv_own, inv_other, pair_send.at[1], pair_recv.at[1], chip, 1 - core)

    def step(phase, q, hop, src, dst):
        stride = ORDERS[q % 3][(0, 1, 2, 1, 0, 0, 0)[phase]]
        at = (0, 1, 2, 3, 4, 1, 4)[phase] * CHAINS + q
        return remote(src, dst, ring_send.at[q], ring_recv.at[at], partner(chip, stride, hop), core)

    def piece_rows(at, piece):
        turn = coordinate(chip, ORDERS[at // 4 % 3][1])
        return rows_at(at * TILE + (piece - turn + 4) % 4 * FINE, FINE)

    def chunk_start(q, hop=0):
        return q * PART + (coordinate(chip, ORDERS[q % 3][0]) + hop) % 4 * CHUNK

    def own_rows(q, hop=0):
        return rows_at(chunk_start(q, hop), FINE)

    def further_rows(q, hop=0):
        return rows_at(chunk_start(q, hop) + FINE, 3 * FINE)

    def first(q, hop):
        return step(0, q, hop, part.at[further_rows(q, hop), :], got_a.at[q, hop - 1, FINE:CHUNK])

    def first_own(q, hop):
        return step(5, q, hop, part.at[own_rows(q, hop), :], got_a.at[q, hop - 1, 0:FINE])

    def second(q, hop):
        return step(1, q, hop, sum_a.at[q, hop * FINE:(hop + 1) * FINE, :], got_b.at[q, hop - 1])

    def third(q, hop):
        return step(2, q, hop, sum_b.at[q], got_c.at[q, hop - 1])

    def fourth(q, hop):
        landing = rows_at(chunk_start(q) + (4 - hop) * FINE, FINE)
        return step(3, q, hop, full.at[own_rows(q), :], full.at[landing, :])

    def fourth_own(q, hop):
        return step(6, q, hop, full.at[own_rows(q), :], full.at[own_rows(q), :])

    def fifth(q, hop):
        return step(4, q, hop, full.at[further_rows(q), :], full.at[further_rows(q), :])

    def chains(wave):
        return range(3 * wave, 3 * wave + 3)

    def start(phase, q):
        for hop in HOPS:
            phase(q, hop).start()

    def waits(phase, q, pieces):
        rows = part.at[0:pieces * FINE, :]
        return remote(rows, rows, ring_send.at[q], ring_recv.at[phase * CHAINS + q], chip, core)

    def arrived(phase, q):
        waits(phase, q, (9, 6, 3, 3, 12)[phase]).wait_recv()

    def summed(*terms):
        total = terms[0].astype(F32)
        for term in terms[1:]:
            total = total + term.astype(F32)
        return total.astype(BF16)


    def sent_in():
        @pl.when(mine)
        def _():
            for copy in all_in(CHIPS - 1):
                copy.wait_send()

        @pl.when(not_mine)
        def _():
            for copy in all_in(CHIPS):
                copy.wait_send()

    swap.start()
    swap_inv.start()

    for wave in range(WAVES):
        blocks = list(enumerate(BLOCKS))[wave * 36 // WAVES:(wave + 1) * 36 // WAVES]
        for r in range(8):
            columns = [c for _, (row, c) in blocks if row == r]
            if columns:
                panel = lax.dot_general(
                    own[r * TILE:(r + 1) * TILE, :], own[columns[0] * TILE:(columns[-1] + 1) * TILE, :],
                    (((1,), (1,)), ((), ())), preferred_element_type=F32,
                )
                for at, (row, c) in blocks:
                    if row == r:
                        block = panel[:, (c - columns[0]) * TILE:(c - columns[0] + 1) * TILE].astype(BF16)
                        for k in range(4):
                            part[piece_rows(at, k), :] = block[k * FINE:(k + 1) * FINE, :]
        for q in chains(wave):
            start(first, q)
    for q in range(CHAINS):
        start(first_own, q)

    sent_in()
    swap.wait()
    swap_inv.wait()
    scale_copy.wait()
    scale = scale_ref[0]
    corr = jnp.sum(own[...].astype(F32) * other[...].astype(F32), axis=0, keepdims=True) / SAMPLES
    diagonal = scale * (2.0 * (corr - 1.0) - 2.0 * offdiag_weight * corr)

    for q in range(CHAINS):
        arrived(0, q)
        further = slice(FINE, CHUNK)
        sum_a[q, further] = summed(part[further_rows(q), :], *(got_a[q, k, further] for k in range(3)))
        start(second, q)
    for q in range(CHAINS):
        arrived(1, q)
        sum_b[q] = summed(part[own_rows(q), :], *(got_a[q, k, 0:FINE] for k in range(3)), *(got_b[q, k] for k in range(3)))
        start(third, q)
    for q in range(CHAINS):
        arrived(2, q)
        full[own_rows(q), :] = summed(sum_b[q], *(got_c[q, k] for k in range(3)))
        start(fourth, q)
        start(fourth_own, q)
    for q in range(CHAINS):
        arrived(3, q)
        start(fifth, q)

    for wave in range(WAVES):
        for q in chains(wave):
            arrived(4, q)
        for at, (r, c) in list(enumerate(BLOCKS))[wave * 36 // WAVES:(wave + 1) * 36 // WAVES]:
            block = jnp.concatenate([full[piece_rows(at, k), :] for k in range(4)], axis=0)
            gram[r * TILE:(r + 1) * TILE, c * TILE:(c + 1) * TILE] = block
            if r != c:
                gram[c * TILE:(c + 1) * TILE, r * TILE:(r + 1) * TILE] = block.T
        since, until = WHOLE[wave], WHOLE[wave + 1]
        rows = jnp.dot(gram[since:until, since:], other[since:, :], preferred_element_type=F32)
        products[since:until, :] = rows if wave == 0 else products[since:until, :] + rows
        if until < SAMPLES:
            rest = jnp.dot(gram[until:, since:until], other[since:until, :], preferred_element_type=F32)
            products[until:, :] = rest if wave == 0 else products[until:, :] + rest
    theirs = other[...].astype(F32)
    back = products[...] * (scale * (2.0 * offdiag_weight / (SAMPLES * SAMPLES)))
    back = back + own[...].astype(F32) * (diagonal / SAMPLES)
    weight = jnp.sum(back * theirs, axis=0, keepdims=True) / SAMPLES
    gain = inv_other[0:1, :]

    place = out.at[1 - core, :, lanes_at(tile)]

    def to_samples(chip_to):
        return remote(grads.at[rows_at(chip_to * ROWS, ROWS), :], place, out_send, out_recv, chip_to, half)

    for y in range(4):
        quarter = slice(y * SAMPLES // 4, (y + 1) * SAMPLES // 4)
        grads[quarter, :] = (gain * (back[quarter, :] - theirs[quarter, :] * weight)).astype(BF16)
        for x, z in PLANE[:-1]:
            to_samples(y * 16 + (at_x + x) % 4 * 4 + (at_z + z) % 4).start()
    for dy in (2, 1, 3):
        to_samples(shifted((dy, 0, 0))).start()

    @pl.when(not_mine)
    def _():
        to_samples(chip).start()

    @pl.when(mine)
    def _():
        pltpu.make_async_copy(grads.at[rows_at(chip * ROWS, ROWS), :], place, local_sem.at[0]).start()

    for q in range(CHAINS):
        waits(0, q, 33).wait_send()

    @pl.when(mine)
    def _():
        all_of(grads, (CHIPS - 1) * ROWS, out_send, out_recv).wait()
        pltpu.make_async_copy(grads.at[rows_at(chip * ROWS, ROWS), :], place, local_sem.at[0]).wait()

    @pl.when(not_mine)
    def _():
        all_of(grads, CHIPS * ROWS, out_send, out_recv).wait()


def shards(view_one, view_two, loss_scale):
    hbm = pl.BlockSpec(memory_space=pltpu.HBM)
    out = pl.pallas_call(
        kernel,
        out_shape=jax.ShapeDtypeStruct((2, ROWS, WIDE), BF16),
        in_specs=[hbm, hbm, hbm],
        out_specs=pl.BlockSpec(memory_space=pltpu.VMEM),
        scratch_shapes=[
            pltpu.VMEM((2, ROWS, WIDE), F32),
            pltpu.VMEM((2, WIDE // TILE, 1, TILE), F32),
            pltpu.VMEM((2, WIDE // TILE, ROWS, TILE), BF16),
            pltpu.VMEM((SAMPLES, TILE), BF16),
            pltpu.VMEM((CHIPS, 1, TILE), F32),
            pltpu.VMEM((SAMPLES, TILE), BF16),
            pltpu.VMEM((SAMPLES, TILE), BF16),
            pltpu.VMEM((8, TILE), F32),
            pltpu.VMEM((8, TILE), F32),
            pltpu.VMEM((CHAINS * PART, TILE), BF16),
            pltpu.VMEM((CHAINS, 3, CHUNK, TILE), BF16),
            pltpu.VMEM((CHAINS, CHUNK, TILE), BF16),
            pltpu.VMEM((CHAINS, 3, FINE, TILE), BF16),
            pltpu.VMEM((CHAINS, FINE, TILE), BF16),
            pltpu.VMEM((CHAINS, 3, FINE, TILE), BF16),
            pltpu.VMEM((CHAINS * PART, TILE), BF16),
            pltpu.VMEM((SAMPLES, SAMPLES), BF16),
            pltpu.VMEM((SAMPLES, TILE), F32),
            pltpu.VMEM((SAMPLES, TILE), BF16),
            pltpu.SMEM((1,), F32),
            pltpu.SemaphoreType.DMA,
            pltpu.SemaphoreType.DMA,
            pltpu.SemaphoreType.DMA,
            pltpu.SemaphoreType.DMA,
            pltpu.SemaphoreType.DMA,
            pltpu.SemaphoreType.DMA,
            pltpu.SemaphoreType.DMA((2,)),
            pltpu.SemaphoreType.DMA((2,)),
            pltpu.SemaphoreType.DMA((CHAINS,)),
            pltpu.SemaphoreType.DMA((PHASES * CHAINS,)),
            pltpu.SemaphoreType.DMA((2,)),
            pltpu.SemaphoreType.DMA((2,)),
            pltpu.SemaphoreType.DMA,
        ],
        compiler_params=pltpu.CompilerParams(
            collective_id=0, has_side_effects=True, vmem_limit_bytes=54848 * 1024
        ),
    )(view_one, view_two, loss_scale)
    return out[0].astype(F32), out[1].astype(F32)


def solution(mesh):
    placed = (P("dp", "feat"), P("dp", "feat"), P())
    return jax.shard_map(
        shards,
        mesh=mesh,
        in_specs=placed,
        out_specs=(P("dp", "feat"), P("dp", "feat")),
        check_vma=False,
    )
```
